512 devices in a mesh: seq: 64 (over x, z_lo, y), tensor: 8 (over z_hi, core).
Axes of the slice: x: 4, y: 8, z: 8 (z_hi: 4, z_lo: 2; z = z_hi * 2 + z_lo), core: 2. Of those that a mesh axis runs over, the one named last changes fastest.
Arguments:
- tokens: bfloat16 [2, 8192, 4096], P(None, 'seq', 'tensor'), may hold values from -6 to 6
- in_weight: bfloat16 [4096, 3, 4096], P('seq', None, 'tensor'), may hold values from -0.09375 to 0.09375
- adapter_down_factors: bfloat16 [8, 4096, 16], P(None, 'tensor'), may hold values from -0.09375 to 0.09375
- adapter_up_factors: bfloat16 [8, 16, 3, 4096], P(None, None, None, 'tensor'), may hold values from -1.5 to 1.5
- filters: bfloat16 [4096, 128], P('tensor'), may hold values from -6 to 6
- task_ids: int32 [2], replicated, may hold values from 0 to 7
- window_lengths: int32 [2, 32], replicated, may hold values from 1 to 512, 8192 in all within a row
- out_weight: bfloat16 [4096, 4096], P('tensor', 'seq'), may hold values from -0.75 to 0.75
Outputs:
- embeddings: bfloat16 [2, 32, 4096], P(None, 'tensor', 'seq')
The draws below stay inside these ranges and needn't reach their ends.
Inputs may be any that keep to these rules, and one draw needn't show every extreme that they name: `window_lengths`: each segment's window lengths sum to 8192, and the longest window of each segment has exactly 512 tokens.
All inputs are finite; a program needn't handle non-finite values.
Results may differ from the reference program's by a relative error of at most 0.014.
Values may be sent and summed in bfloat16 or wider, within the bound.
No kernel may reach another device: no remote copies, remote signals or barrier semaphores. Data moves between devices by JAX's collectives and lax.ppermute only.
A program may use at most 128 MiB of HBM per device.

```python
import math
import jax
import jax.numpy as jnp
import numpy as np
from jax import lax

MODEL_FEATURES = 4096
CONV_CHANNELS = 4096
TAPS = 128
ADAPTER_RANK = 16
TASK_ADAPTERS = 8
SEGS = 2
WIN = 32
SEGMENT_LENGTH = 8192
WIN_MOST = 512


def draw_filters(key, part):
    key = jax.random.fold_in(key, 11)
    rate_key, tap_key = jax.random.split(key)
    log_rate = jax.random.uniform(rate_key, (CONV_CHANNELS, 1), jnp.float32, math.log(0.001), math.log(0.1))
    rate = jnp.exp(log_rate)
    tap_pos = jnp.arange(TAPS, dtype=jnp.float32)[None, :]
    decay = jnp.exp(-rate * tap_pos)
    scaling = jnp.sqrt((1.0 - jnp.exp(-2.0 * rate)) / (1.0 - jnp.exp(-2.0 * rate * TAPS)))
    raw_taps = jnp.clip(jax.random.normal(tap_key, (CONV_CHANNELS, TAPS), jnp.float32), -6.0, 6.0)
    return (raw_taps * decay * scaling).astype(jnp.bfloat16)


def steps_of(own_key, extent, cuts, least, top_value):
    factor_of, own = 1.0, jax.random.fold_in(own_key, 6)
    for axis_at, shards_of in cuts:
        steps = jnp.exp(jax.random.uniform(jax.random.fold_in(own, axis_at), (shards_of,), jnp.float32, least / len(cuts), top_value / len(cuts)))
        factor_of = factor_of * jnp.repeat(steps, extent[axis_at] // shards_of).reshape([-1 if axis == axis_at else 1 for axis in range(len(extent))])
    return factor_of


def profile(number_of, total, reach, lean):
    weights = [(1 << 20) // math.isqrt(rank ** lean) + 1 for rank in range(2, number_of + 1)]
    surplus, holding = total - reach - (number_of - 1), [1] * (number_of - 1)
    while surplus > 0:
        movable = [i for i in range(number_of - 1) if holding[i] < reach]
        mass, remaining = sum([weights[i] for i in movable]), surplus
        for i in movable:
            extra = min(reach - holding[i], max(1, remaining * weights[i] // mass), surplus)
            holding[i] = holding[i] + extra
            surplus = surplus - extra
    return np.array([reach] + holding)


def ragged_sizes(own_key, count, total, most, skew):
    if count == 2:
        one = jax.random.randint(own_key, (), max(1, total - most), min(most, total - 1) + 1)
        return jnp.stack([one, total - one])
    tallies = jnp.asarray(profile(count, total, most, skew), jnp.int32)
    couples = (count - 1) // 2
    donor, taker = tallies[1:1 + 2 * couples:2], tallies[2:2 + 2 * couples:2]
    margin = jnp.minimum(donor - 1, most - taker)
    moved = jax.random.randint(jax.random.fold_in(own_key, 1), (couples,), 0, 1 << 20) % (margin + 1)
    tallies = tallies.at[1:1 + 2 * couples:2].set(donor - moved).at[2:2 + 2 * couples:2].set(taker + moved)
    return tallies[jax.random.permutation(jax.random.fold_in(own_key, 2), count)]


def gaussian(key, extent, deviation, reach, cuts=(), held_as=jnp.bfloat16):
    drawn = deviation * jax.random.normal(key, extent, jnp.float32)
    if cuts:
        drawn = drawn * steps_of(key, extent, cuts, -0.22, 0.18)
    return jnp.clip(drawn, -reach, reach).astype(held_as)


def setup_inputs(seed: int = 0) -> dict:
    seeds = jax.random.split(jax.random.key(seed), 9)
    return {
        "tokens": gaussian(seeds[0], (SEGS, SEGMENT_LENGTH, MODEL_FEATURES), 1.0, 6.0, ((1, 64), (2, 8))),
        "in_weight": gaussian(seeds[1], (MODEL_FEATURES, 3, CONV_CHANNELS), MODEL_FEATURES ** -0.5, 0.09375, ((0, 64), (2, 8))),
        "adapter_down_factors": gaussian(seeds[2], (TASK_ADAPTERS, MODEL_FEATURES, ADAPTER_RANK), MODEL_FEATURES ** -0.5, 0.09375, ((1, 8),)),
        "adapter_up_factors": gaussian(seeds[3], (TASK_ADAPTERS, ADAPTER_RANK, 3, CONV_CHANNELS), ADAPTER_RANK ** -0.5, 1.5, ((3, 8),)),
        "filters": draw_filters(jax.random.fold_in(seeds[8], 71), 0),
        "task_ids": jax.random.randint(seeds[5], (SEGS,), 0, TASK_ADAPTERS).astype(jnp.int32),
        "window_lengths": jax.vmap(lambda own: ragged_sizes(own, WIN, SEGMENT_LENGTH, WIN_MOST, 1))(jax.random.split(seeds[6], SEGS)).reshape((SEGS, WIN)).astype(jnp.int32),
        "out_weight": gaussian(seeds[7], (CONV_CHANNELS, MODEL_FEATURES), (CONV_CHANNELS // 64) ** -0.5, 0.75, ((0, 8), (1, 64))),
    }


adapter_scale = 0.5


def conv_block(kv_block, filter_block):
    length = kv_block.shape[0]
    padded_len = 2 * length
    spectrum = jnp.fft.rfft(kv_block.astype(jnp.float32), n=padded_len, axis=0)
    kernel_spectrum = jnp.fft.rfft(filter_block.astype(jnp.float32).T, n=padded_len, axis=0)
    return jnp.fft.irfft(spectrum * kernel_spectrum, n=padded_len, axis=0)[:length].astype(jnp.float32)


def causal_conv(kv_product, filters):
    channels = kv_product.shape[1]
    group_size = min(512, channels)
    blocks = channels // group_size
    kv_groups = jnp.moveaxis(kv_product.reshape(kv_product.shape[0], blocks, group_size), 1, 0)
    filter_groups = filters.reshape(blocks, group_size, filters.shape[1])
    results = lax.map(lambda pair: conv_block(pair[0], pair[1]), (kv_groups, filter_groups))
    return jnp.moveaxis(results, 0, 1).reshape(kv_product.shape[0], channels)


def reference(tokens, in_weight, adapter_down_factors, adapter_up_factors, filters, task_ids, window_lengths, out_weight):
    embeddings = []
    for segment in range(SEGS):
        segment_tokens = tokens[segment]
        task_index = task_ids[segment]
        down_sel = lax.dynamic_index_in_dim(adapter_down_factors, task_index, 0, keepdims=False)
        selected_up_factor = lax.dynamic_index_in_dim(adapter_up_factors, task_index, 0, keepdims=False)
        base_projection_output = jnp.dot(segment_tokens, in_weight.reshape(MODEL_FEATURES, 3 * CONV_CHANNELS), preferred_element_type=jnp.float32)
        low_rank_rows = jnp.dot(segment_tokens, down_sel, preferred_element_type=jnp.float32).astype(jnp.bfloat16)
        lifted_rows = jnp.dot(low_rank_rows, selected_up_factor.reshape(ADAPTER_RANK, 3 * CONV_CHANNELS), preferred_element_type=jnp.float32)
        projected_output = (base_projection_output + adapter_scale * lifted_rows).reshape(SEGMENT_LENGTH, 3, CONV_CHANNELS)
        queries = projected_output[:, 0]
        kv_product = (projected_output[:, 1] * projected_output[:, 2]).astype(jnp.bfloat16)
        conv = causal_conv(kv_product, filters)
        gated = (queries * conv).astype(jnp.bfloat16)
        lengths_row = window_lengths[segment]
        window_ends = jnp.cumsum(lengths_row, dtype=jnp.int32)
        window_starts = window_ends - lengths_row
        positions = jnp.arange(SEGMENT_LENGTH, dtype=jnp.int32)
        membership = ((positions[None, :] >= window_starts[:, None]) & (positions[None, :] < window_ends[:, None])).astype(jnp.bfloat16)
        window_total = jnp.dot(membership, gated, preferred_element_type=jnp.float32)
        averages = (window_total / lengths_row[:, None].astype(jnp.float32)).astype(jnp.bfloat16)
        embeddings.append(jnp.dot(averages, out_weight, preferred_element_type=jnp.float32).astype(jnp.bfloat16))
    return jnp.stack(embeddings)
```

```python
import functools
import jax
import jax.numpy as jnp
from jax import lax
from jax.experimental import pallas as pl
from jax.experimental.pallas import tpu as pltpu
from jax.sharding import Mesh, PartitionSpec as P

AXES = ("xhi", "xlo", "zlo", "y", "zhi", "core")
SIZES = (2, 2, 2, 8, 4, 2)
SEQ = ("xhi", "xlo", "zlo", "y")
TENSOR = ("zhi", "core")
NZ, NY = 8, 8
adapter_scale = 0.5


def flat(x, y, z, c):
    return (((x % 4) * 2 + (z % NZ) % 2) * NY + y % NY) * 8 + ((z % NZ) // 2) * 2 + c


def permute(value, move, keep=lambda x, y, z, c: True):
    pairs = [
        (flat(x, y, z, c), flat(*move(x, y, z, c)))
        for x in range(4)
        for y in range(NY)
        for z in range(NZ)
        for c in range(2)
        if keep(x, y, z, c)
    ]
    return lax.ppermute(value, AXES, pairs)


def z_step(value, step):
    return permute(value, lambda x, y, z, c: (x, y, z + step, c))


def core_swap(value):
    return permute(value, lambda x, y, z, c: (x, y, z, 1 - c))


def x_pair_swap(value):
    return permute(value, lambda x, y, z, c: (x ^ 1, y, z, c))


def nt_dot(a, b):
    return lax.dot_general(a, b, (((1,), (1,)), ((), ())), preferred_element_type=jnp.float32)


def project_kernel(dists, place, *refs):
    n = len(dists)
    pieces = [refs[2 * i : 2 * i + 2] for i in range(n)]
    weight, up, q_ref, kv_ref, acc, low = refs[2 * n :]
    z, zlo, core = place[0], place[1], place[2]
    half = acc.shape[1] // 2
    ranks = up.shape[0]
    started = set()
    for i, (dist, part) in enumerate(dists):
        rel = dist % 2
        zhi = lax.rem(z + dist, NZ) // 2
        for other in range(2):
            piece = pieces[i][other]
            block = zhi * 2 + (core if other == 0 else 1 - core)
            b = weight[:, pl.ds(block, 1)].reshape(NY * weight.shape[2], weight.shape[3])
            halves = (0, 1) if part is None else (part,)
            if piece.shape[0] > half * len(halves):
                down = piece[half * len(halves) :, :]
                down_of = down
            else:
                down_of = pieces[i + 1][other][half:, :]
            for k, xlo in enumerate(halves):
                rows = piece[half * k : half * (k + 1), :]
                at = pl.ds(half * xlo, half)
                prod = jnp.dot(rows, b, preferred_element_type=jnp.float32)
                lprod = nt_dot(rows, down_of)
                if (rel, xlo) in started:
                    acc[rel, at, :] += prod
                    low[rel, at, :] += lprod
                else:
                    started.add((rel, xlo))
                    acc[rel, at, :] = prod
                    low[rel, at, :] = lprod
    seg_rows = q_ref.shape[2]
    ch = q_ref.shape[3]
    for rel in range(2):
        zlo_at = zlo if rel == 0 else 1 - zlo
        for xlo in range(2):
            for seg in range(2):
                at = pl.ds(half * xlo + seg_rows * seg, seg_rows)
                column = lax.broadcasted_iota(jnp.int32, (seg_rows, ranks), 1)
                mine = column // (ranks // 2) == seg
                lowered = jnp.where(mine, low[rel, at, :], 0.0).astype(jnp.bfloat16)
                lifted = jnp.dot(lowered, up[...], preferred_element_type=jnp.float32)
                proj = acc[rel, at, :] + adapter_scale * lifted
                q_ref[xlo * 2 + zlo_at, seg] = proj[:, :ch]
                kv = proj[:, ch : 2 * ch] * proj[:, 2 * ch :]
                kv_ref[xlo * 2 + zlo_at, seg] = kv.astype(jnp.bfloat16)


def conv_kernel(place, q_ref, kv_ref, prev_ref, wrap_ref, taps_ref, start_ref, end_ref, out_ref, ext):
    xhi, y = place[0], place[1]
    rows, ch = kv_ref.shape[2], kv_ref.shape[3]
    taps = taps_ref.shape[0]
    out_ref[...] = jnp.zeros_like(out_ref)
    count = out_ref.shape[1]

    def block(n, carry):
        quarter, seg = n // 2, lax.rem(n, 2)
        at = jnp.where(y > 0, quarter, jnp.maximum(quarter - 1, 0))
        before = prev_ref[at, seg].astype(jnp.float32)
        wrapped = wrap_ref[seg].astype(jnp.float32)
        before = jnp.where((y == 0) & (quarter == 0), wrapped, before)
        ext[0, 0:8, :] = jnp.zeros((8, ch), jnp.float32)
        ext[0, 8 : 8 + rows, :] = before
        ext[0, 8 + rows :, :] = kv_ref[quarter, seg].astype(jnp.float32)
        for r in range(1, 8):
            ext[r, 8:, :] = ext[0, 8 - r : 8 - r + 2 * rows, :]
        for half in range(2):
            height = rows // 2
            total = jnp.zeros((height, ch), jnp.float32)
            for r in range(8):
                for s in range(taps // 8):
                    begin = 8 + rows + height * half - 8 * s
                    total = total + taps_ref[8 * s + r, :][None, :] * ext[r, begin : begin + height, :]
            gated = (q_ref[quarter, seg, height * half : height * (half + 1), :] * total).astype(jnp.bfloat16)
            x = xhi * 2 + quarter // 2
            base = ((x * 2 + lax.rem(quarter, 2)) * NY + y) * rows + height * half
            position = base + lax.broadcasted_iota(jnp.int32, (count, height), 1)
            inside = (position >= start_ref[seg]) & (position < end_ref[seg])
            member = inside.astype(jnp.float32).astype(jnp.bfloat16)
            out_ref[seg] += jnp.dot(member, gated, preferred_element_type=jnp.float32)
        return carry

    lax.fori_loop(0, 8, block, 0)


VMEM = pl.BlockSpec(memory_space=pltpu.VMEM)
SMEM = pl.BlockSpec(memory_space=pltpu.SMEM)


def local(tokens, in_weight, down_factors, up_factors, filters, task_ids, window_lengths, out_weight):
    segs, rows, depth = tokens.shape
    w_rows, _, channels = in_weight.shape
    ch = channels // 4
    xhi, xlo, zlo, y, zhi, core = (lax.axis_index(name) for name in AXES)
    quarter = xlo * 2 + zlo
    z = zhi * 2 + zlo

    by_quarter = in_weight.reshape(w_rows, 3, 4, ch).transpose(2, 0, 1, 3).reshape(4, w_rows, 3 * ch)
    spread = jnp.concatenate([by_quarter, by_quarter], axis=0)
    met = lax.all_to_all(spread, ("xhi", "xlo", "zlo"), 0, 0, tiled=True)
    weight = lax.all_gather(met, "y", axis=0, tiled=False)

    down = jnp.concatenate(
        [lax.dynamic_index_in_dim(down_factors, task_ids[s], 0, keepdims=False).T for s in range(segs)]
    )
    own = tokens.reshape(segs * rows, depth)
    other = x_pair_swap(own)
    first = xlo == 0
    piece = jnp.concatenate([jnp.where(first, own, other), jnp.where(first, other, own), down])
    half = segs * rows
    dists, held = [(0, None)], [piece]
    ahead = back = piece
    for step in range(1, NZ // 2):
        ahead, back = z_step(ahead, 1), z_step(back, -1)
        dists += [(NZ - step, None), (step, None)]
        held += [ahead, back]
    dists += [(NZ // 2, 0), (NZ // 2, 1)]
    held += [z_step(ahead[:half], 1), z_step(back[half:], -1)]
    swapped = [core_swap(h) for h in held]

    up = jnp.concatenate(
        [lax.dynamic_index_in_dim(up_factors, task_ids[s], 0, keepdims=False) for s in range(segs)]
    )
    up = lax.dynamic_slice_in_dim(up, quarter * ch, ch, 2).reshape(up.shape[0], 3 * ch)
    place = jnp.stack([z, zlo, core]).astype(jnp.int32)
    q, kv = pl.pallas_call(
        functools.partial(project_kernel, dists),
        out_shape=(
            jax.ShapeDtypeStruct((4, segs, rows, ch), jnp.float32),
            jax.ShapeDtypeStruct((4, segs, rows, ch), jnp.bfloat16),
        ),
        in_specs=[SMEM] + [VMEM] * (2 * len(held) + 2),
        out_specs=(VMEM, VMEM),
        scratch_shapes=[
            pltpu.VMEM((2, 2 * half, 3 * ch), jnp.float32),
            pltpu.VMEM((2, 2 * half, up.shape[0]), jnp.float32),
        ],
        compiler_params=pltpu.CompilerParams(vmem_limit_bytes=40 << 20),
        name="project",
    )(place, *[ref for pair in zip(held, swapped) for ref in pair], weight, up)

    prev = permute(kv, lambda x, y, z, c: (x, y + 1, z, c))
    wrap = lax.ppermute(
        kv[3],
        AXES,
        [
            (flat(xl, NY - 1, zz, c), flat(2 + xl, 0, zz, c))
            for xl in range(2)
            for zz in range(NZ)
            for c in range(2)
        ],
    )
    taps = lax.dynamic_slice_in_dim(filters, quarter * ch, ch, 0).astype(jnp.float32).T
    ends = jnp.cumsum(window_lengths, axis=1, dtype=jnp.int32)
    starts = ends - window_lengths
    windows = window_lengths.shape[1]
    total = pl.pallas_call(
        conv_kernel,
        out_shape=jax.ShapeDtypeStruct((segs, windows, ch), jnp.float32),
        in_specs=[SMEM] + [VMEM] * 7,
        out_specs=VMEM,
        scratch_shapes=[pltpu.VMEM((8, 8 + 2 * rows, ch), jnp.float32)],
        compiler_params=pltpu.CompilerParams(vmem_limit_bytes=24 << 20),
        name="conv_pool",
    )(jnp.stack([xhi, y]).astype(jnp.int32), q, kv, prev, wrap, taps, starts[:, :, None], ends[:, :, None])

    count = segs * windows
    parts = lax.all_to_all(total.reshape(count, ch), SEQ, 0, 0, tiled=True)
    summed = parts.reshape(2, 4, NY, ch).sum(axis=(0, 2)).reshape(channels)
    mine = lax.axis_index(SEQ)
    length = lax.dynamic_index_in_dim(window_lengths.reshape(count), mine, 0, keepdims=False)
    means = (summed / length.astype(jnp.float32)).astype(jnp.bfloat16)
    means = lax.all_to_all(jnp.broadcast_to(means[None], (count, channels)), SEQ, 0, 0, tiled=True)
    terms = jnp.dot(means, out_weight, preferred_element_type=jnp.float32)
    out_cols = out_weight.shape[1]
    terms = terms.reshape(segs, 8, windows // 8, out_cols).transpose(1, 0, 2, 3)
    terms = lax.all_to_all(terms, TENSOR, 0, 0, tiled=True)
    return terms.sum(axis=0).astype(jnp.bfloat16)


def solution(mesh):
    fine = Mesh(mesh.devices.reshape(SIZES), AXES)
    in_specs = (
        P(None, SEQ, TENSOR),
        P(SEQ, None, TENSOR),
        P(None, TENSOR, None),
        P(None, None, None, TENSOR),
        P(TENSOR, None),
        P(),
        P(),
        P(TENSOR, SEQ),
    )
    return jax.shard_map(local, mesh=fine, in_specs=in_specs, out_specs=P(None, TENSOR, SEQ), check_vma=False)
```

```python
import functools
import jax
import jax.numpy as jnp
from jax import lax
from jax.experimental import pallas as pl
from jax.experimental.pallas import tpu as pltpu
from jax.sharding import Mesh, PartitionSpec as P

AXES = ("xhi", "xlo", "zlo", "y", "zhi", "core")
SIZES = (2, 2, 2, 8, 4, 2)
SEQ = ("xhi", "xlo", "zlo", "y")
TENSOR = ("zhi", "core")
NZ, NY = 8, 8
adapter_scale = 0.5


def flat(x, y, z, c):
    return (((x % 4) * 2 + (z % NZ) % 2) * NY + y % NY) * 8 + ((z % NZ) // 2) * 2 + c


def permute(value, move, keep=lambda x, y, z, c: True):
    pairs = [
        (flat(x, y, z, c), flat(*move(x, y, z, c)))
        for x in range(4)
        for y in range(NY)
        for z in range(NZ)
        for c in range(2)
        if keep(x, y, z, c)
    ]
    return lax.ppermute(value, AXES, pairs)


def z_step(value, step):
    return permute(value, lambda x, y, z, c: (x, y, z + step, c))


def core_swap(value):
    return permute(value, lambda x, y, z, c: (x, y, z, 1 - c))


def x_pair_swap(value):
    return permute(value, lambda x, y, z, c: (x ^ 1, y, z, c))


def nt_dot(a, b):
    return lax.dot_general(a, b, (((1,), (1,)), ((), ())), preferred_element_type=jnp.float32)


def pieces_of(refs):
    return [refs[2 * d : 2 * d + 2] for d in range(NZ)]


def distances(rel):
    return [d for d in range(NZ) if d % 2 == rel]


def stacked_weight(weight, z, rel, side, columns):
    blocks = []
    for dist in distances(rel):
        zhi = lax.rem(z + dist, NZ) // 2
        block = weight[:, side, pl.ds(zhi, 1), :, columns]
        blocks.append(block.reshape(weight.shape[0] * weight.shape[3], block.shape[-1]))
    return jnp.concatenate(blocks, axis=0)


def stacked_rows(pieces, rel, pair, half):
    return jnp.concatenate([pieces[d][pair][:half, :] for d in distances(rel)], axis=1)


def project_kv_kernel(place, *refs):
    pieces = pieces_of(refs)
    weight, up, up_other, own_ref, send_ref, low_ref = refs[2 * NZ :]
    z = place[0]
    half = own_ref.shape[2]
    ch = up.shape[1] // 3
    ranks = up.shape[0]
    for rel in range(2):
        down = jnp.concatenate([pieces[d][0][half:, :] for d in distances(rel)], axis=1)
        lows = []
        for pair in range(2):
            low = nt_dot(stacked_rows(pieces, rel, pair, half), down)
            row = lax.broadcasted_iota(jnp.int32, (half, ranks), 0)
            column = lax.broadcasted_iota(jnp.int32, (half, ranks), 1)
            mine = (row >= half // 2) == (column >= ranks // 2)
            lows.append(jnp.where(mine, adapter_scale * low, 0.0).astype(jnp.bfloat16))
            low_ref[rel, pair] = lows[pair]
        for side in range(2):
            b = stacked_weight(weight, z, rel, side, slice(ch, 3 * ch))
            ups = (up if side == 0 else up_other)[:, ch:]
            for pair in range(2):
                a = stacked_rows(pieces, rel, pair, half)
                part = jnp.dot(a, b, preferred_element_type=jnp.float32)
                part += jnp.dot(lows[pair], ups, preferred_element_type=jnp.float32)
                if side == 0:
                    own_ref[rel, pair] = part
                else:
                    send_ref[rel, pair] = part.astype(send_ref.dtype)


def project_q_kernel(place, *refs):
    pieces = pieces_of(refs)
    weight, up, up_other, low_ref, own_ref, send_ref = refs[2 * NZ :]
    z = place[0]
    half = own_ref.shape[2]
    ch = up.shape[1] // 3
    for rel in range(2):
        b = jnp.concatenate([stacked_weight(weight, z, rel, side, slice(0, ch)) for side in range(2)], axis=1)
        ups = jnp.concatenate([up[:, :ch], up_other[:, :ch]], axis=1)
        for pair in range(2):
            a = stacked_rows(pieces, rel, pair, half)
            part = jnp.dot(a, b, preferred_element_type=jnp.float32)
            part += jnp.dot(low_ref[rel, pair], ups, preferred_element_type=jnp.float32)
            own_ref[rel, pair] = part[:, :ch]
            send_ref[rel, pair] = part[:, ch:].astype(send_ref.dtype)


def combine_kernel(place, own_ref, met_ref, kv_ref):
    xlo, zlo = place[3], place[1]
    rows, ch = kv_ref.shape[2], kv_ref.shape[3]
    for rel in range(2):
        for pair in range(2):
            quarter = (xlo if pair == 0 else 1 - xlo) * 2 + (zlo if rel == 0 else 1 - zlo)
            both = own_ref[rel, pair] + met_ref[rel, pair].astype(jnp.float32)
            kv = (both[:, :ch] * both[:, ch:]).astype(jnp.bfloat16)
            for seg in range(2):
                kv_ref[quarter, seg] = kv[rows * seg : rows * (seg + 1), :]


def spread_taps(taps_ref, tap, ch):
    return jnp.broadcast_to(taps_ref[tap : tap + 1, :], (8, ch))


def conv_own_kernel(kv_ref, taps_ref, part_ref, ext):
    rows, ch = kv_ref.shape[2], kv_ref.shape[3]
    groups = rows // 8

    def block(n, carry):
        quarter, seg = n // 2, lax.rem(n, 2)
        ext[0:8, :] = jnp.zeros((8, ch), jnp.float32)
        ext[8:, :] = kv_ref[quarter, seg].astype(jnp.float32)
        total = [jnp.zeros((8, ch), jnp.float32) for _ in range(groups)]
        for r in range(8):
            shifted = [ext[8 * g + 8 - r : 8 * g + 16 - r, :] for g in range(groups)]
            for s in range(groups):
                tap = spread_taps(taps_ref, 8 * s + r, ch)
                for g in range(s, groups):
                    total[g] = total[g] + tap * shifted[g - s]
        for g in range(groups):
            part_ref[quarter, seg, 8 * g : 8 * g + 8, :] = total[g]
        return carry

    lax.fori_loop(0, 8, block, 0)


def gate_kernel(place, part_ref, own_ref, met_ref, prev_ref, wrap_ref, taps_ref, start_ref, end_ref, out_ref, ext):
    z_lo, x_lo, x_hi, y = place[1], place[3], place[4], place[5]
    rows, ch = part_ref.shape[2], part_ref.shape[3]
    groups = rows // 8
    count = out_ref.shape[1]
    out_ref[0] = jnp.zeros((count, ch), jnp.float32)
    row = lax.broadcasted_iota(jnp.int32, (count, rows), 0)
    column = lax.broadcasted_iota(jnp.int32, (count, rows), 1)
    row_seg = lax.rem(row // 4, 2)

    def block(n, carry):
        rel, pair, seg = n // 4, lax.rem(n // 2, 2), lax.rem(n, 2)
        z_at = jnp.where(rel == 0, z_lo, 1 - z_lo)
        x_at = jnp.where(pair == 0, x_lo, 1 - x_lo)
        quarter = x_at * 2 + z_at
        at = jnp.where(y > 0, quarter, jnp.maximum(quarter - 1, 0))
        before = prev_ref[at, seg].astype(jnp.float32)
        wrapped = wrap_ref[seg].astype(jnp.float32)
        ext[0:8, :] = jnp.zeros((8, ch), jnp.float32)
        ext[8 : 8 + rows, :] = jnp.where((y == 0) & (quarter == 0), wrapped, before)
        ext[8 + rows :, :] = jnp.zeros((8, ch), jnp.float32)
        total = [part_ref[quarter, seg, 8 * g : 8 * g + 8, :] for g in range(groups)]
        for r in range(8):
            shifted = [ext[8 * g + 8 - r : 8 * g + 16 - r, :] for g in range(groups + (1 if r else 0))]
            for s in range(groups):
                tap = spread_taps(taps_ref, 8 * s + r, ch)
                for g in range(groups):
                    if groups + g - s < len(shifted):
                        total[g] = total[g] + tap * shifted[groups + g - s]
        at_rows = pl.ds(pl.multiple_of(seg * rows, rows), rows)
        q = own_ref[rel, pair, at_rows, :] + met_ref[rel, pair, at_rows, :].astype(jnp.float32)
        gated = (q * jnp.concatenate(total, axis=0)).astype(jnp.bfloat16)
        position = (((x_hi * 2 + x_at) * 2 + z_at) * NY + y) * rows + column
        inside = (position >= start_ref[...]) & (position < end_ref[...]) & (row_seg == seg)
        member = inside.astype(jnp.float32).astype(jnp.bfloat16)
        out_ref[0] += jnp.dot(member, gated, preferred_element_type=jnp.float32)
        return carry

    lax.fori_loop(0, 8, block, 0)
    for copy in range(1, out_ref.shape[0]):
        out_ref[copy] = out_ref[0]


def sum_kernel(met_ref, out_ref):
    total = met_ref[0]
    for i in range(1, met_ref.shape[0]):
        total = total + met_ref[i]
    for copy in range(out_ref.shape[0]):
        out_ref[copy] = total


def embed_kernel(met_ref, length_ref, weight_ref, out_ref):
    length = length_ref[...].astype(jnp.float32)
    means = []
    for t in range(met_ref.shape[2]):
        for quarter in range(met_ref.shape[1]):
            total = met_ref[0, quarter, t] + met_ref[1, quarter, t]
            means.append((total / length).astype(jnp.bfloat16))
    means = jnp.concatenate(means, axis=1)
    weight = weight_ref[...].astype(jnp.bfloat16)
    out_ref[...] = jnp.dot(means, weight, preferred_element_type=jnp.float32).astype(jnp.bfloat16)


VMEM = pl.BlockSpec(memory_space=pltpu.VMEM)
SMEM = pl.BlockSpec(memory_space=pltpu.SMEM)


def call(kernel, name, out, operands, scratch=(), vmem=32, scalars=True):
    return pl.pallas_call(
        kernel,
        out_shape=out,
        in_specs=[SMEM] * scalars + [VMEM] * (len(operands) - scalars),
        out_specs=jax.tree.map(lambda _: VMEM, out),
        scratch_shapes=list(scratch),
        compiler_params=pltpu.CompilerParams(vmem_limit_bytes=vmem << 20),
        name=name,
    )(*operands)


def local(tokens, in_weight, down_factors, up_factors, filters, task_ids, window_lengths, out_weight):
    f32, bf16 = jnp.float32, jnp.bfloat16
    segs, rows, depth = tokens.shape
    w_rows, _, channels = in_weight.shape
    ch = channels // 4
    windows = window_lengths.shape[1]
    xhi, xlo, zlo, y, zhi, core = (lax.axis_index(name) for name in AXES)
    quarter = xlo * 2 + zlo
    z = zhi * 2 + zlo
    place = jnp.stack([z, zlo, core, xlo, xhi, y]).astype(jnp.int32)
    half = segs * rows

    down = jnp.concatenate(
        [lax.dynamic_index_in_dim(down_factors, task_ids[s], 0, keepdims=False).T for s in range(segs)]
    )
    own = tokens.reshape(half, depth)
    other = x_pair_swap(own)
    own = jnp.concatenate([own, down])
    held = {(0, 0): own, (0, 1): other}
    for pair, value in enumerate((own, other)):
        ahead = back = value
        for step in range(1, NZ // 2):
            ahead, back = z_step(ahead, 1), z_step(back, -1)
            held[NZ - step, pair], held[step, pair] = ahead, back
        held[NZ // 2, pair] = z_step(ahead, 1) if pair == 0 else z_step(back, -1)
    pieces = [held[d, pair] for d in range(NZ) for pair in range(2)]

    by_quarter = in_weight.reshape(w_rows, 3, 4, ch).transpose(2, 0, 1, 3).reshape(4, w_rows, 3 * ch)
    met = lax.all_to_all(jnp.concatenate([by_quarter, by_quarter]), ("xhi", "xlo", "zlo"), 0, 0, tiled=True)
    met = met.reshape(4, 2, w_rows, 3 * ch)
    kept = lax.dynamic_index_in_dim(met, core, 1, keepdims=False)
    given = core_swap(lax.dynamic_index_in_dim(met, 1 - core, 1, keepdims=False))
    weight = lax.all_gather(jnp.stack([kept, given]), "y", axis=0, tiled=False)

    up = jnp.concatenate(
        [lax.dynamic_index_in_dim(up_factors, task_ids[s], 0, keepdims=False) for s in range(segs)]
    )
    up = lax.dynamic_slice_in_dim(up, quarter * ch, ch, 2).reshape(up.shape[0], 3 * ch)
    up_other = core_swap(up)
    taps = lax.dynamic_slice_in_dim(filters, quarter * ch, ch, 0).astype(f32).T
    ends = jnp.cumsum(window_lengths, axis=1, dtype=jnp.int32)
    count = segs * windows

    def by_owner(table):
        return table.reshape(segs, 8, windows // 8).transpose(1, 0, 2).reshape(count, 1)

    lengths = by_owner(window_lengths)
    ends = by_owner(ends)
    starts = ends - lengths

    cut = (2, 2, half)
    kv_own, kv_send, low = call(
        project_kv_kernel,
        "project_kv",
        (
            jax.ShapeDtypeStruct((*cut, 2 * ch), f32),
            jax.ShapeDtypeStruct((*cut, 2 * ch), bf16),
            jax.ShapeDtypeStruct((*cut, up.shape[0]), bf16),
        ),
        (place, *pieces, weight, up, up_other),
    )
    kv = call(
        combine_kernel,
        "combine_kv",
        jax.ShapeDtypeStruct((4, segs, rows, ch), bf16),
        (place, kv_own, core_swap(kv_send)),
    )
    prev = permute(kv, lambda x, y, z, c: (x, y + 1, z, c))
    wrap = permute(kv[3], lambda x, y, z, c: (x + 2, 0, z, c), lambda x, y, z, c: x < 2 and y == NY - 1)
    q_own, q_send = call(
        project_q_kernel,
        "project_q",
        (jax.ShapeDtypeStruct((*cut, ch), f32), jax.ShapeDtypeStruct((*cut, ch), bf16)),
        (place, *pieces, weight, up, up_other, low),
    )
    q_met = core_swap(q_send)
    part = call(
        conv_own_kernel,
        "conv_own",
        jax.ShapeDtypeStruct((4, segs, rows, ch), f32),
        (kv, taps),
        [pltpu.VMEM((8 + rows, ch), f32)],
        scalars=False,
    )
    total = call(
        gate_kernel,
        "gate_pool",
        jax.ShapeDtypeStruct((NY, count, ch), f32),
        (place, part, q_own, q_met, prev, wrap, taps, starts, ends),
        [pltpu.VMEM((16 + rows, ch), f32)],
    )

    met = lax.all_to_all(total, "y", 0, 0, tiled=True)
    total = call(sum_kernel, "sum_y", jax.ShapeDtypeStruct((8, count, ch), f32), (met,), scalars=False)
    rest = ("xhi", "xlo", "zlo", "zhi", "core")
    met = lax.all_to_all(total.reshape(64, 8, ch), rest, 0, 0, tiled=True)
    met = met.reshape(2, 4, 8, 8, ch)
    whole = lax.all_gather(out_weight.astype(f32), TENSOR, axis=0, tiled=True)
    mine = lax.dynamic_slice_in_dim(lengths, (zhi * 2 + core) * 8, 8, 0)
    out = call(
        embed_kernel,
        "embed",
        jax.ShapeDtypeStruct((8, out_weight.shape[1]), bf16),
        (met, mine, whole),
        scalars=False,
    )
    return out.reshape(segs, windows // 8, out_weight.shape[1])


def solution(mesh):
    fine = Mesh(mesh.devices.reshape(SIZES), AXES)
    in_specs = (
        P(None, SEQ, TENSOR),
        P(SEQ, None, TENSOR),
        P(None, TENSOR, None),
        P(None, None, None, TENSOR),
        P(TENSOR, None),
        P(),
        P(),
        P(TENSOR, SEQ),
    )
    return jax.shard_map(local, mesh=fine, in_specs=in_specs, out_specs=P(None, TENSOR, SEQ), check_vma=False)
```

```python
import functools
import jax
import jax.numpy as jnp
from jax import lax
from jax.experimental import pallas as pl
from jax.experimental.pallas import tpu as pltpu
from jax.sharding import Mesh, PartitionSpec as P

AXES = ("xhi", "xlo", "zlo", "y", "zhi", "core")
SIZES = (2, 2, 2, 8, 4, 2)
SEQ = ("xhi", "xlo", "zlo", "y")
TENSOR = ("zhi", "core")
NZ, NY = 8, 8
adapter_scale = 0.5


def flat(x, y, z, c):
    return (((x % 4) * 2 + (z % NZ) % 2) * NY + y % NY) * 8 + ((z % NZ) // 2) * 2 + c


def permute(value, move, keep=lambda x, y, z, c: True):
    pairs = [
        (flat(x, y, z, c), flat(*move(x, y, z, c)))
        for x in range(4)
        for y in range(NY)
        for z in range(NZ)
        for c in range(2)
        if keep(x, y, z, c)
    ]
    return lax.ppermute(value, AXES, pairs)


def z_step(value, step):
    return permute(value, lambda x, y, z, c: (x, y, z + step, c))


def core_swap(value):
    return permute(value, lambda x, y, z, c: (x, y, z, 1 - c))


def x_pair_swap(value):
    return permute(value, lambda x, y, z, c: (x ^ 1, y, z, c))


def nt_dot(a, b):
    return lax.dot_general(a, b, (((1,), (1,)), ((), ())), preferred_element_type=jnp.float32)


def fetch(sources, targets, sems):
    copies = [pltpu.make_async_copy(a, b, sems.at[i]) for i, (a, b) in enumerate(zip(sources, targets))]
    for copy in copies:
        copy.start()
    return copies


def targets_of(own_buf, other_buf, weight_buf):
    rows = [buf.at[d] for d in range(NZ) for buf in (own_buf, other_buf)]
    return rows + [weight_buf.at[side] for side in range(2)]


def distances(rel):
    return [d for d in range(NZ) if d % 2 == rel]


def stacked_weight(weight, z, rel, side, columns):
    blocks = []
    for dist in distances(rel):
        zhi = lax.rem(z + dist, NZ) // 2
        block = weight[side, :, pl.ds(zhi, 1), :, columns]
        blocks.append(block.reshape(weight.shape[1] * weight.shape[3], block.shape[-1]))
    return jnp.concatenate(blocks, axis=0)


def stacked_rows(pieces, rel, pair, half):
    return jnp.concatenate([pieces[d][pair][:half, :] for d in distances(rel)], axis=1)


def project_kv_kernel(place, *refs):
    sources = refs[: 2 * NZ + 2]
    up, up_other, own_ref, send_ref, low_ref, own_buf, other_buf, weight, sems = refs[2 * NZ + 2 :]
    for copy in fetch(sources, targets_of(own_buf, other_buf, weight), sems):
        copy.wait()
    pieces = [(own_buf.at[d], other_buf.at[d]) for d in range(NZ)]
    z = place[0]
    half = own_ref.shape[2]
    ch = up.shape[1] // 3
    ranks = up.shape[0]
    for rel in range(2):
        down = jnp.concatenate([pieces[d][0][half:, :] for d in distances(rel)], axis=1)
        lows = []
        for pair in range(2):
            low = nt_dot(stacked_rows(pieces, rel, pair, half), down)
            row = lax.broadcasted_iota(jnp.int32, (half, ranks), 0)
            column = lax.broadcasted_iota(jnp.int32, (half, ranks), 1)
            mine = (row >= half // 2) == (column >= ranks // 2)
            lows.append(jnp.where(mine, adapter_scale * low, 0.0).astype(jnp.bfloat16))
            low_ref[rel, pair] = lows[pair]
        for side in range(2):
            b = stacked_weight(weight, z, rel, side, slice(ch, 3 * ch))
            ups = (up if side == 0 else up_other)[:, ch:]
            for pair in range(2):
                a = stacked_rows(pieces, rel, pair, half)
                part = jnp.dot(a, b, preferred_element_type=jnp.float32)
                part += jnp.dot(lows[pair], ups, preferred_element_type=jnp.float32)
                if side == 0:
                    own_ref[rel, pair] = part
                else:
                    send_ref[rel, pair] = part.astype(send_ref.dtype)


def project_q_kernel(place, *refs):
    sources = refs[: 2 * NZ + 2]
    up, up_other, low_ref, own_ref, send_ref, own_buf, other_buf, weight, sems = refs[2 * NZ + 2 :]
    for copy in fetch(sources, targets_of(own_buf, other_buf, weight), sems):
        copy.wait()
    pieces = [(own_buf.at[d], other_buf.at[d]) for d in range(NZ)]
    z = place[0]
    half = own_ref.shape[2]
    ch = up.shape[1] // 3
    for rel in range(2):
        b = jnp.concatenate([stacked_weight(weight, z, rel, side, slice(0, ch)) for side in range(2)], axis=1)
        ups = jnp.concatenate([up[:, :ch], up_other[:, :ch]], axis=1)
        for pair in range(2):
            a = stacked_rows(pieces, rel, pair, half)
            part = jnp.dot(a, b, preferred_element_type=jnp.float32)
            part += jnp.dot(low_ref[rel, pair], ups, preferred_element_type=jnp.float32)
            own_ref[rel, pair] = part[:, :ch]
            send_ref[rel, pair] = part[:, ch:].astype(send_ref.dtype)


def combine_kernel(place, own_ref, met_ref, kv_ref):
    xlo, zlo = place[3], place[1]
    rows, ch = kv_ref.shape[2], kv_ref.shape[3]
    for rel in range(2):
        for pair in range(2):
            quarter = (xlo if pair == 0 else 1 - xlo) * 2 + (zlo if rel == 0 else 1 - zlo)
            both = own_ref[rel, pair] + met_ref[rel, pair].astype(jnp.float32)
            kv = (both[:, :ch] * both[:, ch:]).astype(jnp.bfloat16)
            for seg in range(2):
                kv_ref[quarter, seg] = kv[rows * seg : rows * (seg + 1), :]


def spread_taps(taps_ref, tap, ch):
    return jnp.broadcast_to(taps_ref[tap : tap + 1, :], (8, ch))


def conv_own_kernel(kv_ref, taps_ref, part_ref, ext):
    rows, ch = kv_ref.shape[2], kv_ref.shape[3]
    groups = rows // 8

    def block(n, carry):
        quarter, seg = n // 2, lax.rem(n, 2)
        ext[0:8, :] = jnp.zeros((8, ch), jnp.float32)
        ext[8:, :] = kv_ref[quarter, seg].astype(jnp.float32)
        total = [jnp.zeros((8, ch), jnp.float32) for _ in range(groups)]
        for r in range(8):
            shifted = [ext[8 * g + 8 - r : 8 * g + 16 - r, :] for g in range(groups)]
            for s in range(groups):
                tap = spread_taps(taps_ref, 8 * s + r, ch)
                for g in range(s, groups):
                    total[g] = total[g] + tap * shifted[g - s]
        for g in range(groups):
            part_ref[quarter, seg, 8 * g : 8 * g + 8, :] = total[g]
        return carry

    lax.fori_loop(0, 8, block, 0)


def gate_kernel(place, part_ref, own_ref, met_ref, prev_ref, wrap_ref, taps_ref, start_ref, end_ref, out_ref, ext, sums):
    z_lo, x_lo, x_hi, y = place[1], place[3], place[4], place[5]
    rows, ch = part_ref.shape[2], part_ref.shape[3]
    groups = rows // 8
    count = out_ref.shape[1]
    sums[...] = jnp.zeros((count, ch), jnp.float32)
    row = lax.broadcasted_iota(jnp.int32, (count, rows), 0)
    column = lax.broadcasted_iota(jnp.int32, (count, rows), 1)
    row_seg = lax.rem(row // 4, 2)

    def block(n, carry):
        rel, pair, seg = n // 4, lax.rem(n // 2, 2), lax.rem(n, 2)
        z_at = jnp.where(rel == 0, z_lo, 1 - z_lo)
        x_at = jnp.where(pair == 0, x_lo, 1 - x_lo)
        quarter = x_at * 2 + z_at
        at = jnp.where(y > 0, quarter, jnp.maximum(quarter - 1, 0))
        before = prev_ref[at, seg].astype(jnp.float32)
        wrapped = wrap_ref[seg].astype(jnp.float32)
        ext[0:8, :] = jnp.zeros((8, ch), jnp.float32)
        ext[8 : 8 + rows, :] = jnp.where((y == 0) & (quarter == 0), wrapped, before)
        ext[8 + rows :, :] = jnp.zeros((8, ch), jnp.float32)
        total = [part_ref[quarter, seg, 8 * g : 8 * g + 8, :] for g in range(groups)]
        for r in range(8):
            shifted = [ext[8 * g + 8 - r : 8 * g + 16 - r, :] for g in range(groups + (1 if r else 0))]
            for s in range(groups):
                tap = spread_taps(taps_ref, 8 * s + r, ch)
                for g in range(groups):
                    if groups + g - s < len(shifted):
                        total[g] = total[g] + tap * shifted[groups + g - s]
        at_rows = pl.ds(pl.multiple_of(seg * rows, rows), rows)
        q = own_ref[rel, pair, at_rows, :] + met_ref[rel, pair, at_rows, :].astype(jnp.float32)
        gated = (q * jnp.concatenate(total, axis=0)).astype(jnp.bfloat16)
        position = (((x_hi * 2 + x_at) * 2 + z_at) * NY + y) * rows + column
        inside = (position >= start_ref[...]) & (position < end_ref[...]) & (row_seg == seg)
        member = inside.astype(jnp.float32).astype(jnp.bfloat16)
        sums[...] += jnp.dot(member, gated, preferred_element_type=jnp.float32)
        return carry

    lax.fori_loop(0, 8, block, 0)
    for copy in range(out_ref.shape[0]):
        out_ref[copy] = sums[...].astype(out_ref.dtype)


def sum_kernel(met_ref, out_ref):
    total = met_ref[0].astype(jnp.float32)
    for i in range(1, met_ref.shape[0]):
        total = total + met_ref[i].astype(jnp.float32)
    for copy in range(out_ref.shape[0]):
        out_ref[copy] = total.astype(out_ref.dtype)


def embed_kernel(met_ref, length_ref, weight_ref, out_ref):
    length = length_ref[...].astype(jnp.float32)
    means = []
    for t in range(met_ref.shape[2]):
        for quarter in range(met_ref.shape[1]):
            total = met_ref[0, quarter, t].astype(jnp.float32) + met_ref[1, quarter, t].astype(jnp.float32)
            means.append((total / length).astype(jnp.bfloat16))
    means = jnp.concatenate(means, axis=1)
    weight = weight_ref[...].astype(jnp.bfloat16)
    out_ref[...] = jnp.dot(means, weight, preferred_element_type=jnp.float32).astype(jnp.bfloat16)


VMEM = pl.BlockSpec(memory_space=pltpu.VMEM)
SMEM = pl.BlockSpec(memory_space=pltpu.SMEM)


ANY = pl.BlockSpec(memory_space=pl.ANY)


def call(kernel, name, out, operands, scratch=(), vmem=24, scalars=True, where=0):
    return pl.pallas_call(
        kernel,
        out_shape=out,
        in_specs=[SMEM] * scalars + [ANY] * where + [VMEM] * (len(operands) - scalars - where),
        out_specs=jax.tree.map(lambda _: VMEM, out),
        scratch_shapes=list(scratch),
        compiler_params=pltpu.CompilerParams(vmem_limit_bytes=vmem << 20),
        name=name,
    )(*operands)


def local(tokens, in_weight, down_factors, up_factors, filters, task_ids, window_lengths, out_weight):
    f32, bf16 = jnp.float32, jnp.bfloat16
    segs, rows, depth = tokens.shape
    w_rows, _, channels = in_weight.shape
    ch = channels // 4
    windows = window_lengths.shape[1]
    xhi, xlo, zlo, y, zhi, core = (lax.axis_index(name) for name in AXES)
    quarter = xlo * 2 + zlo
    z = zhi * 2 + zlo
    place = jnp.stack([z, zlo, core, xlo, xhi, y]).astype(jnp.int32)
    half = segs * rows

    down = jnp.concatenate(
        [lax.dynamic_index_in_dim(down_factors, task_ids[s], 0, keepdims=False).T for s in range(segs)]
    )
    own = tokens.reshape(half, depth)
    other = x_pair_swap(own)
    own = jnp.concatenate([own, down])
    ahead, back = z_step(own, 1), z_step(own, -1)

    by_quarter = in_weight.reshape(w_rows, 3, 4, ch).transpose(2, 0, 1, 3).reshape(4, w_rows, 3 * ch)
    met = lax.all_to_all(jnp.concatenate([by_quarter, by_quarter]), ("xhi", "xlo", "zlo"), 0, 0, tiled=True)
    ahead, back, other, met = lax.optimization_barrier((ahead, back, other, met))
    met = met.reshape(4, 2, w_rows, 3 * ch)
    kept = lax.dynamic_index_in_dim(met, core, 1, keepdims=False)
    given = core_swap(lax.dynamic_index_in_dim(met, 1 - core, 1, keepdims=False))
    weights = [lax.all_gather(side, "y", axis=0, tiled=False) for side in (kept, given)]

    up = jnp.concatenate(
        [lax.dynamic_index_in_dim(up_factors, task_ids[s], 0, keepdims=False) for s in range(segs)]
    )
    up = lax.dynamic_slice_in_dim(up, quarter * ch, ch, 2).reshape(up.shape[0], 3 * ch)
    up_other = core_swap(up)
    taps = lax.dynamic_slice_in_dim(filters, quarter * ch, ch, 0).astype(f32).T
    ends = jnp.cumsum(window_lengths, axis=1, dtype=jnp.int32)
    count = segs * windows

    def by_owner(table):
        return table.reshape(segs, 8, windows // 8).transpose(1, 0, 2).reshape(count, 1)

    lengths = by_owner(window_lengths)
    ends = by_owner(ends)
    starts = ends - lengths
    mine = lax.dynamic_slice_in_dim(lengths, (zhi * 2 + core) * 8, 8, 0)
    wide = out_weight.astype(f32)

    held = {(0, 0): own, (0, 1): other, (NZ - 1, 0): ahead, (1, 0): back}
    held[NZ - 1, 1], held[1, 1] = z_step(other, 1), z_step(other, -1)
    for step in range(2, NZ // 2):
        for pair in range(2):
            held[NZ - step, pair] = z_step(held[NZ - step + 1, pair], 1)
            held[step, pair] = z_step(held[step - 1, pair], -1)
        if step == 2:
            early = [held[NZ - 2, 0], up, up_other, taps, starts, ends, mine, wide, place]
            early = lax.optimization_barrier(early)
            held[NZ - 2, 0], up, up_other, taps, starts, ends, mine, wide, place = early
    held[NZ // 2, 0] = z_step(held[NZ // 2 + 1, 0], 1)
    held[NZ // 2, 1] = z_step(held[NZ // 2 - 1, 1], -1)
    pieces = [held[d, pair] for d in range(NZ) for pair in range(2)]
    *weights, wide = lax.optimization_barrier((*weights, wide))
    whole = lax.all_gather(wide, TENSOR, axis=0, tiled=True)

    cut = (2, 2, half)
    buffers = [
        pltpu.VMEM((NZ, *own.shape), bf16),
        pltpu.VMEM((NZ, *other.shape), bf16),
        pltpu.VMEM((2, *weights[0].shape), bf16),
        pltpu.SemaphoreType.DMA((2 * NZ + 2,)),
    ]
    kv_own, kv_send, low = call(
        project_kv_kernel,
        "project_kv",
        (
            jax.ShapeDtypeStruct((*cut, 2 * ch), f32),
            jax.ShapeDtypeStruct((*cut, 2 * ch), bf16),
            jax.ShapeDtypeStruct((*cut, up.shape[0]), bf16),
        ),
        (place, *pieces, *weights, up, up_other),
        buffers,
        where=len(pieces) + 2,
    )
    kv = call(
        combine_kernel,
        "combine_kv",
        jax.ShapeDtypeStruct((4, segs, rows, ch), bf16),
        (place, kv_own, core_swap(kv_send)),
    )
    prev = permute(kv, lambda x, y, z, c: (x, y + 1, z, c))
    wrap = permute(kv[3], lambda x, y, z, c: (x + 2, 0, z, c), lambda x, y, z, c: x < 2 and y == NY - 1)
    q_own, q_send = call(
        project_q_kernel,
        "project_q",
        (jax.ShapeDtypeStruct((*cut, ch), f32), jax.ShapeDtypeStruct((*cut, ch), bf16)),
        (place, *pieces, *weights, up, up_other, low),
        buffers,
        where=len(pieces) + 2,
    )
    q_met = core_swap(q_send)
    part = call(
        conv_own_kernel,
        "conv_own",
        jax.ShapeDtypeStruct((4, segs, rows, ch), f32),
        (kv, taps),
        [pltpu.VMEM((8 + rows, ch), f32)],
        scalars=False,
    )
    total = call(
        gate_kernel,
        "gate_pool",
        jax.ShapeDtypeStruct((NY, count, ch), bf16),
        (place, part, q_own, q_met, prev, wrap, taps, starts, ends),
        [pltpu.VMEM((16 + rows, ch), f32), pltpu.VMEM((count, ch), f32)],
    )

    met = lax.all_to_all(total, "y", 0, 0, tiled=True)
    total = call(sum_kernel, "sum_y", jax.ShapeDtypeStruct((8, count, ch), bf16), (met,), scalars=False)
    rest = ("xhi", "xlo", "zlo", "zhi", "core")
    total, whole, mine = lax.optimization_barrier((total, whole, mine))
    met = lax.all_to_all(total.reshape(64, 8, ch), rest, 0, 0, tiled=True)
    met = met.reshape(2, 4, 8, 8, ch)
    out = call(
        embed_kernel,
        "embed",
        jax.ShapeDtypeStruct((8, out_weight.shape[1]), bf16),
        (met, mine, whole),
        scalars=False,
    )
    return out.reshape(segs, windows // 8, out_weight.shape[1])


def solution(mesh):
    fine = Mesh(mesh.devices.reshape(SIZES), AXES)
    in_specs = (
        P(None, SEQ, TENSOR),
        P(SEQ, None, TENSOR),
        P(None, TENSOR, None),
        P(None, None, None, TENSOR),
        P(TENSOR, None),
        P(),
        P(),
        P(TENSOR, SEQ),
    )
    return jax.shard_map(local, mesh=fine, in_specs=in_specs, out_specs=P(None, TENSOR, SEQ), check_vma=False)
```

```python
import functools
import jax
import jax.numpy as jnp
from jax import lax
from jax.experimental import pallas as pl
from jax.experimental.pallas import tpu as pltpu
from jax.sharding import Mesh, PartitionSpec as P

AXES = ("xhi", "xlo", "zlo", "y", "zhi", "core")
SIZES = (2, 2, 2, 8, 4, 2)
SEQ = ("xhi", "xlo", "zlo", "y")
TENSOR = ("zhi", "core")
NZ, NY = 8, 8
adapter_scale = 0.5


def flat(x, y, z, c):
    return (((x % 4) * 2 + (z % NZ) % 2) * NY + y % NY) * 8 + ((z % NZ) // 2) * 2 + c


def permute(value, move, keep=lambda x, y, z, c: True):
    pairs = [
        (flat(x, y, z, c), flat(*move(x, y, z, c)))
        for x in range(4)
        for y in range(NY)
        for z in range(NZ)
        for c in range(2)
        if keep(x, y, z, c)
    ]
    return lax.ppermute(value, AXES, pairs)


def y_step(value, step):
    return permute(value, lambda x, y, z, c: (x, y + step, z, c))


def core_swap(value):
    return permute(value, lambda x, y, z, c: (x, y, z, 1 - c))


def x_pair_swap(value):
    return permute(value, lambda x, y, z, c: (x ^ 1, y, z, c))


def nt_dot(a, b):
    return lax.dot_general(a, b, (((1,), (1,)), ((), ())), preferred_element_type=jnp.float32)


def position():
    x_hi, x_lo, z_lo, y, z_hi, core = (lax.axis_index(name) for name in AXES)
    return x_hi, x_lo, z_lo, y, z_hi, core


def fetch(sources, targets, sems):
    copies = [pltpu.make_async_copy(a, b, sems.at[i]) for i, (a, b) in enumerate(zip(sources, targets))]
    for copy in copies:
        copy.start()
    for copy in copies:
        copy.wait()


def stacked_weight(weight, side, columns):
    blocks = [weight[:, side, z_hi, :, columns] for z_hi in range(weight.shape[2])]
    return jnp.concatenate([b.reshape(-1, b.shape[-1]) for b in blocks], axis=0)


def project_kernel(tokens_ref, *refs):
    pieces, refs = refs[:NY], refs[NY:]
    up, up_other, kv_own, kv_send, q_own, q_send, tokens, weight, sems = refs
    copies = [pltpu.make_async_copy(tokens_ref.at[z], tokens.at[z], sems.at[z]) for z in range(NZ)]
    for z_lo in range(2):
        for z in range(z_lo, NZ, 2):
            copies[z].start()
    y = position()[3]
    for dist in range(NY):
        weight[lax.rem(y + dist, NY)] = pieces[dist][...]
    half = kv_own.shape[1]
    ch = up.shape[1] // 3
    ranks = up.shape[0]
    row = lax.broadcasted_iota(jnp.int32, (half, ranks), 0)
    column = lax.broadcasted_iota(jnp.int32, (half, ranks), 1)
    mine = (row >= half // 2) == (column >= ranks // 2)
    kv_columns, q_columns = slice(ch, 3 * ch), slice(0, ch)
    kv_weight = [stacked_weight(weight, side, kv_columns) for side in range(2)]
    q_weight = jnp.concatenate([stacked_weight(weight, side, q_columns) for side in range(2)], axis=1)
    q_up = jnp.concatenate([up[:, q_columns], up_other[:, q_columns]], axis=1)
    for z_lo in range(2):
        for z in range(z_lo, NZ, 2):
            copies[z].wait()
        down = jnp.concatenate([tokens[z, 2 * half :, :] for z in range(z_lo, NZ, 2)], axis=1)
        for x_lo in range(2):
            quarter = x_lo * 2 + z_lo
            rows = [tokens[z, half * x_lo : half * (x_lo + 1), :] for z in range(z_lo, NZ, 2)]
            a = jnp.concatenate(rows, axis=1)
            low = jnp.where(mine, adapter_scale * nt_dot(a, down), 0.0).astype(jnp.bfloat16)
            for side in range(2):
                part = jnp.dot(a, kv_weight[side], preferred_element_type=jnp.float32)
                ups = (up if side == 0 else up_other)[:, kv_columns]
                part += jnp.dot(low, ups, preferred_element_type=jnp.float32)
                if side == 0:
                    kv_own[quarter] = part
                else:
                    kv_send[quarter] = part.astype(kv_send.dtype)
            part = jnp.dot(a, q_weight, preferred_element_type=jnp.float32)
            part += jnp.dot(low, q_up, preferred_element_type=jnp.float32)
            q_own[quarter] = part[:, :ch]
            q_send[quarter] = part[:, ch:].astype(q_send.dtype)


def combine_kernel(own_ref, met_ref, kv_ref):
    rows, ch = kv_ref.shape[2], kv_ref.shape[3]
    for quarter in range(4):
        both = own_ref[quarter] + met_ref[quarter].astype(jnp.float32)
        kv = (both[:, :ch] * both[:, ch:]).astype(jnp.bfloat16)
        for seg in range(2):
            kv_ref[quarter, seg] = kv[rows * seg : rows * (seg + 1), :]


def prepare_kernel(tasks, down_ref, up_ref, down_out, up_out, sems):
    _, x_lo, z_lo, _, _, _ = position()
    ranks = down_ref.shape[1]
    ch = up_out.shape[1] // 3
    columns = pl.ds(pl.multiple_of((x_lo * 2 + z_lo) * ch, ch), ch)
    pairs = []
    for seg in range(2):
        at = pl.ds(seg * ranks, ranks)
        pairs.append((down_ref.at[tasks[seg]], down_out.at[at]))
        for stream in range(3):
            pairs.append((up_ref.at[tasks[seg], stream, :, columns], up_out.at[at, pl.ds(stream * ch, ch)]))
    fetch(*zip(*pairs), sems)


def join_kernel(own_ref, other_ref, down_ref, out_ref):
    x_lo = position()[1]
    half = own_ref.shape[0]
    out_ref[pl.ds(pl.multiple_of(x_lo * half, half), half), :] = own_ref[...]
    out_ref[pl.ds(pl.multiple_of((1 - x_lo) * half, half), half), :] = other_ref[...]
    out_ref[2 * half :, :] = down_ref[...]


def split_kernel(met_ref, kept_ref, given_ref):
    core = position()[5]
    for block in range(kept_ref.shape[0]):
        kept_ref[block] = met_ref[2 * block + core]
        given_ref[block] = met_ref[2 * block + 1 - core]


def spread_kernel(weight_ref, out_ref):
    ch = out_ref.shape[2] // 3
    for quarter in range(4):
        for stream in range(3):
            block = weight_ref[stream, :, quarter * ch : (quarter + 1) * ch]
            for copy in range(2):
                out_ref[copy * 4 + quarter, :, stream * ch : (stream + 1) * ch] = block


def spread_taps(taps_ref, tap, ch):
    return jnp.broadcast_to(taps_ref[tap : tap + 1, :], (8, ch))


def fill_taps(filters_ref, taps):
    _, x_lo, z_lo, _, _, _ = position()
    ch = taps.shape[1]
    mine = filters_ref[pl.ds(pl.multiple_of((x_lo * 2 + z_lo) * ch, ch), ch), :]
    taps[...] = mine.astype(jnp.float32).T


def conv_own_kernel(kv_ref, filters_ref, part_ref, ext, taps):
    rows, ch = kv_ref.shape[2], kv_ref.shape[3]
    groups = rows // 8
    fill_taps(filters_ref, taps)

    def block(n, carry):
        quarter, seg = n // 2, lax.rem(n, 2)
        ext[0:8, :] = jnp.zeros((8, ch), jnp.float32)
        ext[8:, :] = kv_ref[quarter, seg].astype(jnp.float32)
        total = [jnp.zeros((8, ch), jnp.float32) for _ in range(groups)]
        for r in range(8):
            shifted = [ext[8 * g + 8 - r : 8 * g + 16 - r, :] for g in range(groups)]
            for s in range(groups):
                tap = spread_taps(taps, 8 * s + r, ch)
                for g in range(s, groups):
                    total[g] = total[g] + tap * shifted[g - s]
        for g in range(groups):
            part_ref[quarter, seg, 8 * g : 8 * g + 8, :] = total[g]
        return carry

    lax.fori_loop(0, 8, block, 0)


def gate_kernel(lengths, part_ref, own_ref, met_ref, prev_ref, wrap_ref, filters_ref, out_ref, ext, sums, taps, edges):
    x_hi, _, _, y, _, _ = position()
    rows, ch = part_ref.shape[2], part_ref.shape[3]
    groups = rows // 8
    count = out_ref.shape[1]
    each = lengths.shape[1] // 8
    fill_taps(filters_ref, taps)
    for seg in range(2):
        start = jnp.int32(0)
        for window in range(lengths.shape[1]):
            at = (window // each) * 2 * each + seg * each + window % each
            end = start + lengths[seg, window]
            edges[0, at : at + 1, :] = jnp.full((1, rows), start, jnp.int32)
            edges[1, at : at + 1, :] = jnp.full((1, rows), end, jnp.int32)
            start = end
    sums[...] = jnp.zeros((count, ch), jnp.float32)
    row = lax.broadcasted_iota(jnp.int32, (count, rows), 0)
    column = lax.broadcasted_iota(jnp.int32, (count, rows), 1)
    row_seg = lax.rem(row // each, 2)

    def block(n, carry):
        quarter, seg = n // 2, lax.rem(n, 2)
        at = jnp.where(y > 0, quarter, jnp.maximum(quarter - 1, 0))
        before = prev_ref[at, seg].astype(jnp.float32)
        wrapped = wrap_ref[seg].astype(jnp.float32)
        ext[0:8, :] = jnp.zeros((8, ch), jnp.float32)
        ext[8 : 8 + rows, :] = jnp.where((y == 0) & (quarter == 0), wrapped, before)
        ext[8 + rows :, :] = jnp.zeros((8, ch), jnp.float32)
        total = [part_ref[quarter, seg, 8 * g : 8 * g + 8, :] for g in range(groups)]
        for r in range(8):
            shifted = [ext[8 * g + 8 - r : 8 * g + 16 - r, :] for g in range(groups + (1 if r else 0))]
            for s in range(groups):
                tap = spread_taps(taps, 8 * s + r, ch)
                for g in range(groups):
                    if groups + g - s < len(shifted):
                        total[g] = total[g] + tap * shifted[groups + g - s]
        at_rows = pl.ds(pl.multiple_of(seg * rows, rows), rows)
        q = own_ref[quarter, at_rows, :] + met_ref[quarter, at_rows, :].astype(jnp.float32)
        gated = (q * jnp.concatenate(total, axis=0)).astype(jnp.bfloat16)
        place = ((x_hi * 4 + quarter) * NY + y) * rows + column
        inside = (place >= edges[0]) & (place < edges[1]) & (row_seg == seg)
        member = inside.astype(jnp.float32).astype(jnp.bfloat16)
        sums[...] += jnp.dot(member, gated, preferred_element_type=jnp.float32)
        return carry

    lax.fori_loop(0, 8, block, 0)
    for copy in range(out_ref.shape[0]):
        out_ref[copy] = sums[...].astype(out_ref.dtype)


def sum_kernel(met_ref, out_ref):
    total = met_ref[0].astype(jnp.float32)
    for i in range(1, met_ref.shape[0]):
        total = total + met_ref[i].astype(jnp.float32)
    for copy in range(out_ref.shape[0]):
        out_ref[copy] = total.astype(out_ref.dtype)


def embed_kernel(lengths, met_ref, weight_ref, out_ref):
    _, _, _, _, z_hi, core = position()
    rows, ch = met_ref.shape[3], met_ref.shape[4]
    each = rows // 2
    row = lax.broadcasted_iota(jnp.int32, (rows, ch), 0)
    length = jnp.zeros((rows, ch), jnp.int32)
    for r in range(rows):
        length = jnp.where(row == r, lengths[r // each, (z_hi * 2 + core) * each + r % each], length)
    length = length.astype(jnp.float32)
    columns = weight_ref.shape[0] // met_ref.shape[2]
    total = jnp.zeros((rows, columns), jnp.float32)
    for t in range(met_ref.shape[2]):
        means = []
        for quarter in range(met_ref.shape[1]):
            both = met_ref[0, quarter, t].astype(jnp.float32) + met_ref[1, quarter, t].astype(jnp.float32)
            means.append((both / length).astype(jnp.bfloat16))
        weight = weight_ref[t * columns : (t + 1) * columns, :].astype(jnp.bfloat16)
        total += nt_dot(jnp.concatenate(means, axis=1), weight)
    out_ref[...] = total.astype(out_ref.dtype)


VMEM = pl.BlockSpec(memory_space=pltpu.VMEM)
SMEM = pl.BlockSpec(memory_space=pltpu.SMEM)


ANY = pl.BlockSpec(memory_space=pltpu.HBM)


def call(kernel, name, out, operands, scratch=(), vmem=24, scalars=False, where=0):
    return pl.pallas_call(
        kernel,
        out_shape=out,
        in_specs=[SMEM] * scalars + [ANY] * where + [VMEM] * (len(operands) - scalars - where),
        out_specs=jax.tree.map(lambda _: VMEM, out),
        scratch_shapes=list(scratch),
        compiler_params=pltpu.CompilerParams(vmem_limit_bytes=vmem << 20),
        name=name,
    )(*operands)


def local(tokens, in_weight, down_factors, up_factors, filters, task_ids, window_lengths, out_weight):
    f32, bf16 = jnp.float32, jnp.bfloat16
    segs, rows, depth = tokens.shape
    w_rows, _, channels = in_weight.shape
    ch = channels // 4
    windows = window_lengths.shape[1]
    ranks = segs * down_factors.shape[2]
    half = segs * rows
    count = segs * windows

    down, up = call(
        prepare_kernel,
        "adapters",
        (jax.ShapeDtypeStruct((ranks, depth), bf16), jax.ShapeDtypeStruct((ranks, 3 * ch), bf16)),
        (task_ids, down_factors.transpose(0, 2, 1), up_factors.transpose(0, 2, 1, 3)),
        [pltpu.SemaphoreType.DMA((8,))],
        scalars=True,
        where=2,
    )
    own = tokens.reshape(half, depth)
    other = x_pair_swap(own)
    piece = call(
        join_kernel, "join_rows", jax.ShapeDtypeStruct((2 * half + ranks, depth), bf16), (own, other, down)
    )
    gathered = lax.all_gather(piece, ("zhi", "zlo"), axis=0, tiled=False)

    spread = call(
        spread_kernel,
        "spread_weight",
        jax.ShapeDtypeStruct((8, w_rows, 3 * ch), bf16),
        (in_weight.transpose(1, 0, 2),),
    )
    spread, piece = lax.optimization_barrier((spread, piece))
    met = lax.all_to_all(spread, ("xhi", "xlo", "zlo"), 0, 0, tiled=True)
    split = jax.ShapeDtypeStruct((4, w_rows, 3 * ch), bf16)
    kept, given = call(split_kernel, "split_rows", (split, split), (met,))
    weight = {0: jnp.stack([kept, core_swap(given)])}
    for step in range(1, NY // 2):
        weight[NY - step] = y_step(weight[(NY - step + 1) % NY], 1)
        weight[step] = y_step(weight[step - 1], -1)
    weight[NY // 2] = y_step(weight[NY // 2 + 1], 1)
    up_other = core_swap(up)

    cut = (4, half)
    kv_own, kv_send, q_own, q_send = call(
        project_kernel,
        "project",
        (
            jax.ShapeDtypeStruct((*cut, 2 * ch), f32),
            jax.ShapeDtypeStruct((*cut, 2 * ch), bf16),
            jax.ShapeDtypeStruct((*cut, ch), f32),
            jax.ShapeDtypeStruct((*cut, ch), bf16),
        ),
        (gathered, *[weight[d] for d in range(NY)], up, up_other),
        [
            pltpu.VMEM(gathered.shape, bf16),
            pltpu.VMEM((NY, *weight[0].shape), bf16),
            pltpu.SemaphoreType.DMA((NZ,)),
        ],
        vmem=48,
        where=1,
    )
    kv = call(
        combine_kernel,
        "combine_kv",
        jax.ShapeDtypeStruct((4, segs, rows, ch), bf16),
        (kv_own, core_swap(kv_send)),
    )
    prev = permute(kv, lambda x, y, z, c: (x, y + 1, z, c))
    wrap = permute(kv[3], lambda x, y, z, c: (x + 2, 0, z, c), lambda x, y, z, c: x < 2 and y == NY - 1)
    q_met = core_swap(q_send)
    part = call(
        conv_own_kernel,
        "conv_own",
        jax.ShapeDtypeStruct((4, segs, rows, ch), f32),
        (kv, filters),
        [pltpu.VMEM((8 + rows, ch), f32), pltpu.VMEM((filters.shape[1], ch), f32)],
    )
    total = call(
        gate_kernel,
        "gate_pool",
        jax.ShapeDtypeStruct((NY, count, ch), bf16),
        (window_lengths, part, q_own, q_met, prev, wrap, filters),
        [
            pltpu.VMEM((16 + rows, ch), f32),
            pltpu.VMEM((count, ch), f32),
            pltpu.VMEM((filters.shape[1], ch), f32),
            pltpu.VMEM((2, count, rows), jnp.int32),
        ],
        scalars=True,
    )

    met = lax.all_to_all(total, "y", 0, 0, tiled=True)
    total = call(sum_kernel, "sum_y", jax.ShapeDtypeStruct((8, count, ch), bf16), (met,))
    rest = ("xhi", "xlo", "zlo", "zhi", "core")
    met = lax.all_to_all(total.reshape(64, 8, ch), rest, 0, 0, tiled=True)
    met = met.reshape(2, 4, 8, 8, ch)
    wide, kv_send = lax.optimization_barrier((out_weight.T.astype(f32), kv_send))
    whole = lax.all_gather(wide, TENSOR, axis=0, tiled=True)
    out = call(
        embed_kernel,
        "embed",
        jax.ShapeDtypeStruct((8, out_weight.shape[1]), bf16),
        (window_lengths, met, whole),
        scalars=True,
    )
    return out.reshape(segs, windows // 8, out_weight.shape[1])


def solution(mesh):
    fine = Mesh(mesh.devices.reshape(SIZES), AXES)
    in_specs = (
        P(None, SEQ, TENSOR),
        P(SEQ, None, TENSOR),
        P(None, TENSOR, None),
        P(None, None, None, TENSOR),
        P(TENSOR, None),
        P(),
        P(),
        P(TENSOR, SEQ),
    )
    return jax.shard_map(local, mesh=fine, in_specs=in_specs, out_specs=P(None, TENSOR, SEQ), check_vma=False)
```

```python
import functools
import jax
import jax.numpy as jnp
from jax import lax
from jax.experimental import pallas as pl
from jax.experimental.pallas import tpu as pltpu
from jax.sharding import Mesh, PartitionSpec as P

AXES = ("xhi", "xlo", "zlo", "y", "zhi", "core")
SIZES = (2, 2, 2, 8, 4, 2)
SEQ = ("xhi", "xlo", "zlo", "y")
TENSOR = ("zhi", "core")
NZ, NY = 8, 8
adapter_scale = 0.5


def flat(x, y, z, c):
    return (((x % 4) * 2 + (z % NZ) % 2) * NY + y % NY) * 8 + ((z % NZ) // 2) * 2 + c


def permute(value, move, keep=lambda x, y, z, c: True):
    pairs = [
        (flat(x, y, z, c), flat(*move(x, y, z, c)))
        for x in range(4)
        for y in range(NY)
        for z in range(NZ)
        for c in range(2)
        if keep(x, y, z, c)
    ]
    return lax.ppermute(value, AXES, pairs)


def y_step(value, step):
    return permute(value, lambda x, y, z, c: (x, y + step, z, c))


def core_swap(value):
    return permute(value, lambda x, y, z, c: (x, y, z, 1 - c))


def x_pair_swap(value):
    return permute(value, lambda x, y, z, c: (x ^ 1, y, z, c))


def nt_dot(a, b):
    return lax.dot_general(a, b, (((1,), (1,)), ((), ())), preferred_element_type=jnp.float32)


def position():
    x_hi, x_lo, z_lo, y, z_hi, core = (lax.axis_index(name) for name in AXES)
    return x_hi, x_lo, z_lo, y, z_hi, core


def fetch(sources, targets, sems):
    copies = [pltpu.make_async_copy(a, b, sems.at[i]) for i, (a, b) in enumerate(zip(sources, targets))]
    for copy in copies:
        copy.start()
    for copy in copies:
        copy.wait()


def rows_of(tokens, quarter, half):
    x_lo, z_lo = quarter // 2, quarter % 2
    return jnp.concatenate([tokens[z, half * x_lo : half * (x_lo + 1), :] for z in range(z_lo, NZ, 2)], axis=1)


def place_rows(target, piece, y):
    _, blocks, w_rows, columns = piece.shape
    ch = columns // 3
    for block in range(blocks):
        at = pl.ds(pl.multiple_of((block * NY + y) * w_rows, w_rows), w_rows)
        for side in range(2):
            target[side, at, :] = piece[side, block, :, ch:]
            target[2, at, side * ch : (side + 1) * ch] = piece[side, block, :, :ch]


def pack_kernel(*refs):
    count = NY - 1
    out_ref, held, sems = refs[count:]
    copies = [pltpu.make_async_copy(refs[i], held.at[i], sems.at[i]) for i in range(count)]
    for copy in copies:
        copy.start()
    for i, dist in enumerate(d for d in range(NY) if d != NY // 2):
        copies[i].wait()
        place_rows(out_ref, held.at[i], lax.rem(position()[3] + dist, NY))


def project_kernel(tokens, packed, last, up, up_other, kv_own, kv_send, q_own, q_send, weight):
    weight[...] = packed[...]
    place_rows(weight, last, lax.rem(position()[3] + NY // 2, NY))
    half = kv_own.shape[1]
    ch = up.shape[1] // 3
    ranks = up.shape[0]
    row = lax.broadcasted_iota(jnp.int32, (half, ranks), 0)
    column = lax.broadcasted_iota(jnp.int32, (half, ranks), 1)
    mine = (row >= half // 2) == (column >= ranks // 2)
    q_up = jnp.concatenate([up[:, :ch], up_other[:, :ch]], axis=1)
    lows = {}
    for quarter in (0, 2, 1, 3):
        z_lo = quarter % 2
        down = jnp.concatenate([tokens[z, 2 * half :, :] for z in range(z_lo, NZ, 2)], axis=1)
        a = rows_of(tokens, quarter, half)
        low = jnp.where(mine, adapter_scale * nt_dot(a, down), 0.0).astype(jnp.bfloat16)
        lows[quarter] = low
        for side in range(2):
            part = jnp.dot(a, weight[side], preferred_element_type=jnp.float32)
            ups = (up if side == 0 else up_other)[:, ch:]
            part += jnp.dot(low, ups, preferred_element_type=jnp.float32)
            if side == 0:
                kv_own[quarter] = part
            else:
                kv_send[quarter] = part.astype(kv_send.dtype)
    for quarter in range(4):
        part = jnp.dot(rows_of(tokens, quarter, half), weight[2], preferred_element_type=jnp.float32)
        part += jnp.dot(lows[quarter], q_up, preferred_element_type=jnp.float32)
        q_own[quarter] = part[:, :ch]
        q_send[quarter] = part[:, ch:].astype(q_send.dtype)


def combine_kernel(own_ref, met_ref, kv_ref):
    rows, ch = kv_ref.shape[2], kv_ref.shape[3]
    for quarter in range(4):
        both = own_ref[quarter] + met_ref[quarter].astype(jnp.float32)
        kv = (both[:, :ch] * both[:, ch:]).astype(jnp.bfloat16)
        for seg in range(2):
            kv_ref[quarter, seg] = kv[rows * seg : rows * (seg + 1), :]


def prepare_kernel(tasks, down_ref, up_ref, down_out, up_out, sems):
    _, x_lo, z_lo, _, _, _ = position()
    ranks = down_ref.shape[1]
    ch = up_out.shape[1] // 3
    columns = pl.ds(pl.multiple_of((x_lo * 2 + z_lo) * ch, ch), ch)
    pairs = []
    for seg in range(2):
        at = pl.ds(seg * ranks, ranks)
        pairs.append((down_ref.at[tasks[seg]], down_out.at[at]))
        for stream in range(3):
            pairs.append((up_ref.at[tasks[seg], stream, :, columns], up_out.at[at, pl.ds(stream * ch, ch)]))
    fetch(*zip(*pairs), sems)


def join_kernel(own_ref, other_ref, down_ref, out_ref):
    x_lo = position()[1]
    half = own_ref.shape[0]
    out_ref[pl.ds(pl.multiple_of(x_lo * half, half), half), :] = own_ref[...]
    out_ref[pl.ds(pl.multiple_of((1 - x_lo) * half, half), half), :] = other_ref[...]
    out_ref[2 * half :, :] = down_ref[...]


def split_kernel(met_ref, kept_ref, given_ref):
    core = position()[5]
    for block in range(kept_ref.shape[0]):
        kept_ref[block] = met_ref[2 * block + core]
        given_ref[block] = met_ref[2 * block + 1 - core]


def spread_kernel(weight_ref, out_ref):
    ch = out_ref.shape[2] // 3
    for quarter in range(4):
        for stream in range(3):
            block = weight_ref[stream, :, quarter * ch : (quarter + 1) * ch]
            for copy in range(2):
                out_ref[copy * 4 + quarter, :, stream * ch : (stream + 1) * ch] = block


def spread_taps(taps_ref, tap, ch):
    return jnp.broadcast_to(taps_ref[tap : tap + 1, :], (8, ch))


def fill_taps(filters_ref, taps):
    _, x_lo, z_lo, _, _, _ = position()
    ch = taps.shape[1]
    mine = filters_ref[pl.ds(pl.multiple_of((x_lo * 2 + z_lo) * ch, ch), ch), :]
    taps[...] = mine.astype(jnp.float32).T


def conv_own_kernel(kv_ref, filters_ref, part_ref, ext, taps):
    rows, ch = kv_ref.shape[2], kv_ref.shape[3]
    groups = rows // 8
    fill_taps(filters_ref, taps)

    def block(n, carry):
        quarter, seg = n // 2, lax.rem(n, 2)
        ext[0:8, :] = jnp.zeros((8, ch), jnp.float32)
        ext[8:, :] = kv_ref[quarter, seg].astype(jnp.float32)
        total = [jnp.zeros((8, ch), jnp.float32) for _ in range(groups)]
        for r in range(8):
            shifted = [ext[8 * g + 8 - r : 8 * g + 16 - r, :] for g in range(groups)]
            for s in range(groups):
                tap = spread_taps(taps, 8 * s + r, ch)
                for g in range(s, groups):
                    total[g] = total[g] + tap * shifted[g - s]
        for g in range(groups):
            part_ref[quarter, seg, 8 * g : 8 * g + 8, :] = total[g]
        return carry

    lax.fori_loop(0, 8, block, 0)


def gate_kernel(lengths, part_ref, own_ref, met_ref, prev_ref, wrap_ref, filters_ref, out_ref, ext, sums, taps, edges):
    x_hi, _, _, y, _, _ = position()
    rows, ch = part_ref.shape[2], part_ref.shape[3]
    groups = rows // 8
    count = out_ref.shape[1]
    each = lengths.shape[1] // 8
    fill_taps(filters_ref, taps)
    for seg in range(2):
        start = jnp.int32(0)
        for window in range(lengths.shape[1]):
            at = (window // each) * 2 * each + seg * each + window % each
            end = start + lengths[seg, window]
            edges[0, at : at + 1, :] = jnp.full((1, rows), start, jnp.int32)
            edges[1, at : at + 1, :] = jnp.full((1, rows), end, jnp.int32)
            start = end
    sums[...] = jnp.zeros((count, ch), jnp.float32)
    row = lax.broadcasted_iota(jnp.int32, (count, rows), 0)
    column = lax.broadcasted_iota(jnp.int32, (count, rows), 1)
    row_seg = lax.rem(row // each, 2)

    def block(n, carry):
        quarter, seg = n // 2, lax.rem(n, 2)
        at = jnp.where(y > 0, quarter, jnp.maximum(quarter - 1, 0))
        before = prev_ref[at, seg].astype(jnp.float32)
        wrapped = wrap_ref[seg].astype(jnp.float32)
        ext[0:8, :] = jnp.zeros((8, ch), jnp.float32)
        ext[8 : 8 + rows, :] = jnp.where((y == 0) & (quarter == 0), wrapped, before)
        ext[8 + rows :, :] = jnp.zeros((8, ch), jnp.float32)
        total = [part_ref[quarter, seg, 8 * g : 8 * g + 8, :] for g in range(groups)]
        for r in range(8):
            shifted = [ext[8 * g + 8 - r : 8 * g + 16 - r, :] for g in range(groups + (1 if r else 0))]
            for s in range(groups):
                tap = spread_taps(taps, 8 * s + r, ch)
                for g in range(groups):
                    if groups + g - s < len(shifted):
                        total[g] = total[g] + tap * shifted[groups + g - s]
        at_rows = pl.ds(pl.multiple_of(seg * rows, rows), rows)
        q = own_ref[quarter, at_rows, :] + met_ref[quarter, at_rows, :].astype(jnp.float32)
        gated = (q * jnp.concatenate(total, axis=0)).astype(jnp.bfloat16)
        place = ((x_hi * 4 + quarter) * NY + y) * rows + column
        inside = (place >= edges[0]) & (place < edges[1]) & (row_seg == seg)
        member = inside.astype(jnp.float32).astype(jnp.bfloat16)
        sums[...] += jnp.dot(member, gated, preferred_element_type=jnp.float32)
        return carry

    lax.fori_loop(0, 8, block, 0)
    for copy in range(out_ref.shape[0]):
        out_ref[copy] = sums[...].astype(out_ref.dtype)


def sum_kernel(met_ref, out_ref):
    total = met_ref[0].astype(jnp.float32)
    for i in range(1, met_ref.shape[0]):
        total = total + met_ref[i].astype(jnp.float32)
    rows = out_ref.shape[2]
    for place in range(out_ref.shape[0]):
        mine = total[place * rows : (place + 1) * rows, :].astype(out_ref.dtype)
        for copy in range(out_ref.shape[1]):
            out_ref[place, copy] = mine


def embed_kernel(lengths, met_ref, weight_ref, out_ref):
    _, _, _, _, z_hi, core = position()
    rows, ch = met_ref.shape[3], met_ref.shape[4]
    each = rows // 2
    row = lax.broadcasted_iota(jnp.int32, (rows, ch), 0)
    length = jnp.zeros((rows, ch), jnp.int32)
    for r in range(rows):
        length = jnp.where(row == r, lengths[r // each, (z_hi * 2 + core) * each + r % each], length)
    length = length.astype(jnp.float32)
    columns = weight_ref.shape[0] // met_ref.shape[0]
    total = jnp.zeros((rows, columns), jnp.float32)
    for t in range(met_ref.shape[0]):
        means = []
        for quarter in range(met_ref.shape[2]):
            both = met_ref[t, 0, quarter].astype(jnp.float32) + met_ref[t, 1, quarter].astype(jnp.float32)
            means.append((both / length).astype(jnp.bfloat16))
        weight = weight_ref[t * columns : (t + 1) * columns, :].astype(jnp.bfloat16)
        total += nt_dot(jnp.concatenate(means, axis=1), weight)
    out_ref[...] = total.astype(out_ref.dtype)


VMEM = pl.BlockSpec(memory_space=pltpu.VMEM)
SMEM = pl.BlockSpec(memory_space=pltpu.SMEM)


ANY = pl.BlockSpec(memory_space=pltpu.HBM)


def call(kernel, name, out, operands, scratch=(), vmem=24, scalars=False, where=0):
    return pl.pallas_call(
        kernel,
        out_shape=out,
        in_specs=[SMEM] * scalars + [ANY] * where + [VMEM] * (len(operands) - scalars - where),
        out_specs=jax.tree.map(lambda _: VMEM, out),
        scratch_shapes=list(scratch),
        compiler_params=pltpu.CompilerParams(vmem_limit_bytes=vmem << 20),
        name=name,
    )(*operands)


def local(tokens, in_weight, down_factors, up_factors, filters, task_ids, window_lengths, out_weight):
    f32, bf16 = jnp.float32, jnp.bfloat16
    segs, rows, depth = tokens.shape
    w_rows, _, channels = in_weight.shape
    ch = channels // 4
    windows = window_lengths.shape[1]
    ranks = segs * down_factors.shape[2]
    half = segs * rows
    count = segs * windows

    down, up = call(
        prepare_kernel,
        "adapters",
        (jax.ShapeDtypeStruct((ranks, depth), bf16), jax.ShapeDtypeStruct((ranks, 3 * ch), bf16)),
        (task_ids, down_factors.transpose(0, 2, 1), up_factors.transpose(0, 2, 1, 3)),
        [pltpu.SemaphoreType.DMA((8,))],
        scalars=True,
        where=2,
    )
    own = tokens.reshape(half, depth)
    other = x_pair_swap(own)
    piece = call(
        join_kernel, "join_rows", jax.ShapeDtypeStruct((2 * half + ranks, depth), bf16), (own, other, down)
    )
    gathered = lax.all_gather(piece, ("zhi", "zlo"), axis=0, tiled=False)

    spread = call(
        spread_kernel,
        "spread_weight",
        jax.ShapeDtypeStruct((8, w_rows, 3 * ch), bf16),
        (in_weight.transpose(1, 0, 2),),
    )
    spread, piece = lax.optimization_barrier((spread, piece))
    met = lax.all_to_all(spread, ("xhi", "xlo", "zlo"), 0, 0, tiled=True)
    split = jax.ShapeDtypeStruct((4, w_rows, 3 * ch), bf16)
    kept, given = call(split_kernel, "split_rows", (split, split), (met,))
    weight = {0: jnp.stack([kept, core_swap(given)])}
    for step in range(1, NY // 2):
        weight[NY - step] = y_step(weight[(NY - step + 1) % NY], 1)
        weight[step] = y_step(weight[step - 1], -1)
    weight[NY // 2] = y_step(weight[NY // 2 + 1], 1)
    up_other = core_swap(up)

    cut = (4, half)
    features = w_rows * NY * 4
    early = [weight[d] for d in range(NY) if d != NY // 2]
    gathered, *early = lax.optimization_barrier((gathered, *early))
    packed = call(
        pack_kernel,
        "pack_weights",
        jax.ShapeDtypeStruct((3, features, 2 * ch), bf16),
        tuple(early),
        [pltpu.VMEM((NY - 1, *weight[0].shape), bf16), pltpu.SemaphoreType.DMA((NY - 1,))],
        vmem=56,
        where=NY - 1,
    )
    kv_own, kv_send, q_own, q_send = call(
        project_kernel,
        "project",
        (
            jax.ShapeDtypeStruct((*cut, 2 * ch), f32),
            jax.ShapeDtypeStruct((*cut, 2 * ch), bf16),
            jax.ShapeDtypeStruct((*cut, ch), f32),
            jax.ShapeDtypeStruct((*cut, ch), bf16),
        ),
        (gathered, packed, weight[NY // 2], up, up_other),
        [pltpu.VMEM(packed.shape, bf16)],
    )
    kv = call(
        combine_kernel,
        "combine_kv",
        jax.ShapeDtypeStruct((4, segs, rows, ch), bf16),
        (kv_own, core_swap(kv_send)),
    )
    wide, kv = lax.optimization_barrier((out_weight.T.astype(f32), kv))
    whole = lax.all_gather(wide, TENSOR, axis=0, tiled=True)
    prev = permute(kv, lambda x, y, z, c: (x, y + 1, z, c))
    wrap = permute(kv[3], lambda x, y, z, c: (x + 2, 0, z, c), lambda x, y, z, c: x < 2 and y == NY - 1)
    q_met = core_swap(q_send)
    part = call(
        conv_own_kernel,
        "conv_own",
        jax.ShapeDtypeStruct((4, segs, rows, ch), f32),
        (kv, filters),
        [pltpu.VMEM((8 + rows, ch), f32), pltpu.VMEM((filters.shape[1], ch), f32)],
    )
    total = call(
        gate_kernel,
        "gate_pool",
        jax.ShapeDtypeStruct((NY, count, ch), bf16),
        (window_lengths, part, q_own, q_met, prev, wrap, filters),
        [
            pltpu.VMEM((16 + rows, ch), f32),
            pltpu.VMEM((count, ch), f32),
            pltpu.VMEM((filters.shape[1], ch), f32),
            pltpu.VMEM((2, count, rows), jnp.int32),
        ],
        scalars=True,
    )

    met = lax.all_to_all(total, "y", 0, 0, tiled=True)
    total = call(sum_kernel, "sum_y", jax.ShapeDtypeStruct((8, 8, 8, ch), bf16), (met,))
    rest = TENSOR + ("xhi", "xlo", "zlo")
    met = lax.all_to_all(total.reshape(64, 8, ch), rest, 0, 0, tiled=True)
    met = met.reshape(8, 2, 4, 8, ch)
    out = call(
        embed_kernel,
        "embed",
        jax.ShapeDtypeStruct((8, out_weight.shape[1]), bf16),
        (window_lengths, met, whole),
        scalars=True,
    )
    return out.reshape(segs, windows // 8, out_weight.shape[1])


def solution(mesh):
    fine = Mesh(mesh.devices.reshape(SIZES), AXES)
    in_specs = (
        P(None, SEQ, TENSOR),
        P(SEQ, None, TENSOR),
        P(None, TENSOR, None),
        P(None, None, None, TENSOR),
        P(TENSOR, None),
        P(),
        P(),
        P(TENSOR, SEQ),
    )
    return jax.shard_map(local, mesh=fine, in_specs=in_specs, out_specs=P(None, TENSOR, SEQ), check_vma=False)
```

```python
import functools
import jax
import jax.numpy as jnp
from jax import lax
from jax.experimental import pallas as pl
from jax.experimental.pallas import tpu as pltpu
from jax.sharding import Mesh, PartitionSpec as P

AXES = ("xhi", "xlo", "zlo", "y", "zhi", "core")
SIZES = (2, 2, 2, 8, 4, 2)
SEQ = ("xhi", "xlo", "zlo", "y")
TENSOR = ("zhi", "core")
NZ, NY = 8, 8
adapter_scale = 0.5


def flat(x, y, z, c):
    return (((x % 4) * 2 + (z % NZ) % 2) * NY + y % NY) * 8 + ((z % NZ) // 2) * 2 + c


def permute(value, move, keep=lambda x, y, z, c: True):
    pairs = [
        (flat(x, y, z, c), flat(*move(x, y, z, c)))
        for x in range(4)
        for y in range(NY)
        for z in range(NZ)
        for c in range(2)
        if keep(x, y, z, c)
    ]
    return lax.ppermute(value, AXES, pairs)


def y_step(value, step):
    return permute(value, lambda x, y, z, c: (x, y + step, z, c))


def core_swap(value):
    return permute(value, lambda x, y, z, c: (x, y, z, 1 - c))


def x_pair_swap(value):
    return permute(value, lambda x, y, z, c: (x ^ 1, y, z, c))


def nt_dot(a, b):
    return lax.dot_general(a, b, (((1,), (1,)), ((), ())), preferred_element_type=jnp.float32)


def position():
    x_hi, x_lo, z_lo, y, z_hi, core = (lax.axis_index(name) for name in AXES)
    return x_hi, x_lo, z_lo, y, z_hi, core


def fetch(sources, targets, sems):
    copies = [pltpu.make_async_copy(a, b, sems.at[i]) for i, (a, b) in enumerate(zip(sources, targets))]
    for copy in copies:
        copy.start()
    for copy in copies:
        copy.wait()


def rows_of(tokens, quarter, half):
    x_lo, z_lo = quarter // 2, quarter % 2
    return jnp.concatenate([tokens[z, half * x_lo : half * (x_lo + 1), :] for z in range(z_lo, NZ, 2)], axis=1)


def place_rows(target, piece, y):
    _, blocks, w_rows, columns = piece.shape
    ch = columns // 3
    for block in range(blocks):
        at = pl.ds(pl.multiple_of((block * NY + y) * w_rows, w_rows), w_rows)
        for side in range(2):
            target[side, at, :] = piece[side, block, :, ch:]
            target[2, at, side * ch : (side + 1) * ch] = piece[side, block, :, :ch]


def pack_kernel(*refs):
    count = NY - 1
    out_ref, held, sems = refs[count:]
    copies = [pltpu.make_async_copy(refs[i], held.at[i], sems.at[i]) for i in range(count)]
    for copy in copies:
        copy.start()
    for i, dist in enumerate(d for d in range(NY) if d != NY // 2):
        copies[i].wait()
        place_rows(out_ref, held.at[i], lax.rem(position()[3] + dist, NY))


def low_kernel(tokens, low_ref):
    _, half, ranks = low_ref.shape
    row = lax.broadcasted_iota(jnp.int32, (half, ranks), 0)
    column = lax.broadcasted_iota(jnp.int32, (half, ranks), 1)
    mine = (row >= half // 2) == (column >= ranks // 2)
    for quarter in range(4):
        down = jnp.concatenate([tokens[z, 2 * half :, :] for z in range(quarter % 2, NZ, 2)], axis=1)
        low = nt_dot(rows_of(tokens, quarter, half), down)
        low_ref[quarter] = jnp.where(mine, adapter_scale * low, 0.0).astype(low_ref.dtype)


def project_kernel(tokens, packed, last, low_ref, up, up_other, kv_own, kv_send, q_own, q_send, weight):
    weight[...] = packed[...]
    place_rows(weight, last, lax.rem(position()[3] + NY // 2, NY))
    half = kv_own.shape[1]
    ch = up.shape[1] // 3
    q_up = jnp.concatenate([up[:, :ch], up_other[:, :ch]], axis=1)
    for quarter in (0, 2, 1, 3):
        a = rows_of(tokens, quarter, half)
        low = low_ref[quarter]
        for side in range(2):
            part = jnp.dot(a, weight[side], preferred_element_type=jnp.float32)
            ups = (up if side == 0 else up_other)[:, ch:]
            part += jnp.dot(low, ups, preferred_element_type=jnp.float32)
            if side == 0:
                kv_own[quarter] = part
            else:
                kv_send[quarter] = part.astype(kv_send.dtype)
    for quarter in range(4):
        part = jnp.dot(rows_of(tokens, quarter, half), weight[2], preferred_element_type=jnp.float32)
        part += jnp.dot(low_ref[quarter], q_up, preferred_element_type=jnp.float32)
        q_own[quarter] = part[:, :ch]
        q_send[quarter] = part[:, ch:].astype(q_send.dtype)


def combine_kernel(own_ref, met_ref, kv_ref):
    rows, ch = kv_ref.shape[2], kv_ref.shape[3]
    for quarter in range(4):
        both = own_ref[quarter] + met_ref[quarter].astype(jnp.float32)
        kv = (both[:, :ch] * both[:, ch:]).astype(jnp.bfloat16)
        for seg in range(2):
            kv_ref[quarter, seg] = kv[rows * seg : rows * (seg + 1), :]


def prepare_kernel(tasks, down_ref, up_ref, down_out, up_out, sems):
    _, x_lo, z_lo, _, _, _ = position()
    ranks = down_ref.shape[1]
    ch = up_out.shape[1] // 3
    columns = pl.ds(pl.multiple_of((x_lo * 2 + z_lo) * ch, ch), ch)
    pairs = []
    for seg in range(2):
        at = pl.ds(seg * ranks, ranks)
        pairs.append((down_ref.at[tasks[seg]], down_out.at[at]))
        for stream in range(3):
            pairs.append((up_ref.at[tasks[seg], stream, :, columns], up_out.at[at, pl.ds(stream * ch, ch)]))
    fetch(*zip(*pairs), sems)


def join_kernel(own_ref, other_ref, down_ref, out_ref):
    x_lo = position()[1]
    half = own_ref.shape[0]
    out_ref[pl.ds(pl.multiple_of(x_lo * half, half), half), :] = own_ref[...]
    out_ref[pl.ds(pl.multiple_of((1 - x_lo) * half, half), half), :] = other_ref[...]
    out_ref[2 * half :, :] = down_ref[...]


def split_kernel(met_ref, kept_ref, given_ref):
    core = position()[5]
    for block in range(kept_ref.shape[0]):
        kept_ref[block] = met_ref[2 * block + core]
        given_ref[block] = met_ref[2 * block + 1 - core]


def spread_kernel(weight_ref, out_ref):
    ch = out_ref.shape[2] // 3
    for quarter in range(4):
        for stream in range(3):
            block = weight_ref[stream, :, quarter * ch : (quarter + 1) * ch]
            for copy in range(2):
                out_ref[copy * 4 + quarter, :, stream * ch : (stream + 1) * ch] = block


def spread_taps(taps_ref, tap, ch):
    return jnp.broadcast_to(taps_ref[tap : tap + 1, :], (8, ch))


def fill_taps(filters_ref, taps):
    _, x_lo, z_lo, _, _, _ = position()
    ch = taps.shape[1]
    mine = filters_ref[pl.ds(pl.multiple_of((x_lo * 2 + z_lo) * ch, ch), ch), :]
    taps[...] = mine.astype(jnp.float32).T


def conv_own_kernel(kv_ref, filters_ref, part_ref, ext, taps):
    rows, ch = kv_ref.shape[2], kv_ref.shape[3]
    groups = rows // 8
    fill_taps(filters_ref, taps)

    def block(n, carry):
        quarter, seg = n // 2, lax.rem(n, 2)
        ext[0:8, :] = jnp.zeros((8, ch), jnp.float32)
        ext[8:, :] = kv_ref[quarter, seg].astype(jnp.float32)
        total = [jnp.zeros((8, ch), jnp.float32) for _ in range(groups)]
        for r in range(8):
            shifted = [ext[8 * g + 8 - r : 8 * g + 16 - r, :] for g in range(groups)]
            for s in range(groups):
                tap = spread_taps(taps, 8 * s + r, ch)
                for g in range(s, groups):
                    total[g] = total[g] + tap * shifted[g - s]
        for g in range(groups):
            part_ref[quarter, seg, 8 * g : 8 * g + 8, :] = total[g]
        return carry

    lax.fori_loop(0, 8, block, 0)


def fill_edges(lengths, edges):
    each = lengths.shape[1] // 8
    for seg in range(2):
        start = jnp.int32(0)
        for window in range(lengths.shape[1]):
            at = (window // each) * 2 * each + seg * each + window % each
            end = start + lengths[seg, window]
            edges[0, at : at + 1, :] = jnp.full((1, edges.shape[2]), start, jnp.int32)
            edges[1, at : at + 1, :] = jnp.full((1, edges.shape[2]), end, jnp.int32)
            start = end


def gate_block(quarter, seg, before, part_ref, own_ref, met_ref, taps, edges, ext, sums):
    x_hi, _, _, y, _, _ = position()
    rows, ch = part_ref.shape[2], part_ref.shape[3]
    groups = rows // 8
    count = sums.shape[0]
    row = lax.broadcasted_iota(jnp.int32, (count, rows), 0)
    column = lax.broadcasted_iota(jnp.int32, (count, rows), 1)
    row_seg = lax.rem(row // 4, 2)
    ext[0:8, :] = jnp.zeros((8, ch), jnp.float32)
    ext[8 : 8 + rows, :] = before.astype(jnp.float32)
    ext[8 + rows :, :] = jnp.zeros((8, ch), jnp.float32)
    total = [part_ref[quarter, seg, 8 * g : 8 * g + 8, :] for g in range(groups)]
    for r in range(8):
        shifted = [ext[8 * g + 8 - r : 8 * g + 16 - r, :] for g in range(groups + (1 if r else 0))]
        for s in range(groups):
            tap = spread_taps(taps, 8 * s + r, ch)
            for g in range(groups):
                if groups + g - s < len(shifted):
                    total[g] = total[g] + tap * shifted[groups + g - s]
    at_rows = pl.ds(pl.multiple_of(seg * rows, rows), rows)
    q = own_ref[quarter, at_rows, :] + met_ref[quarter, at_rows, :].astype(jnp.float32)
    gated = (q * jnp.concatenate(total, axis=0)).astype(jnp.bfloat16)
    place = ((x_hi * 4 + quarter) * NY + y) * rows + column
    inside = (place >= edges[0]) & (place < edges[1]) & (row_seg == seg)
    member = inside.astype(jnp.float32).astype(jnp.bfloat16)
    sums[...] += jnp.dot(member, gated, preferred_element_type=jnp.float32)


def gate_most_kernel(lengths, part_ref, own_ref, met_ref, prev_ref, filters_ref, sums, ext, taps, edges):
    fill_taps(filters_ref, taps)
    fill_edges(lengths, edges)
    sums[...] = jnp.zeros(sums.shape, jnp.float32)
    y = position()[3]

    def block(n, carry):
        quarter, seg = n // 2, lax.rem(n, 2)
        before = prev_ref[jnp.where(y > 0, quarter, quarter - 1), seg]
        gate_block(quarter, seg, before, part_ref, own_ref, met_ref, taps, edges, ext, sums)
        return carry

    lax.fori_loop(2, 8, block, 0)


def gate_first_kernel(
    lengths, most_ref, part_ref, own_ref, met_ref, prev_ref, wrap_ref, filters_ref, out_ref, ext, taps, edges, sums
):
    fill_taps(filters_ref, taps)
    fill_edges(lengths, edges)
    sums[...] = most_ref[...]
    y = position()[3]

    def block(seg, carry):
        before = jnp.where(y > 0, prev_ref[0, seg].astype(jnp.float32), wrap_ref[seg].astype(jnp.float32))
        gate_block(0, seg, before, part_ref, own_ref, met_ref, taps, edges, ext, sums)
        return carry

    lax.fori_loop(0, 2, block, 0)
    for copy in range(out_ref.shape[0]):
        out_ref[copy] = sums[...].astype(out_ref.dtype)


def sum_kernel(met_ref, out_ref):
    total = met_ref[0].astype(jnp.float32)
    for i in range(1, met_ref.shape[0]):
        total = total + met_ref[i].astype(jnp.float32)
    rows = out_ref.shape[2]
    for place in range(out_ref.shape[0]):
        mine = total[place * rows : (place + 1) * rows, :].astype(out_ref.dtype)
        for copy in range(out_ref.shape[1]):
            out_ref[place, copy] = mine


def embed_kernel(lengths, met_ref, weight_ref, out_ref):
    _, _, _, _, z_hi, core = position()
    rows, ch = met_ref.shape[3], met_ref.shape[4]
    each = rows // 2
    row = lax.broadcasted_iota(jnp.int32, (rows, ch), 0)
    length = jnp.zeros((rows, ch), jnp.int32)
    for r in range(rows):
        length = jnp.where(row == r, lengths[r // each, (z_hi * 2 + core) * each + r % each], length)
    length = length.astype(jnp.float32)
    columns = weight_ref.shape[0] // met_ref.shape[0]
    total = jnp.zeros((rows, columns), jnp.float32)
    for t in range(met_ref.shape[0]):
        means = []
        for quarter in range(met_ref.shape[2]):
            both = met_ref[t, 0, quarter].astype(jnp.float32) + met_ref[t, 1, quarter].astype(jnp.float32)
            means.append((both / length).astype(jnp.bfloat16))
        weight = weight_ref[t * columns : (t + 1) * columns, :].astype(jnp.bfloat16)
        total += nt_dot(jnp.concatenate(means, axis=1), weight)
    out_ref[...] = total.astype(out_ref.dtype)


VMEM = pl.BlockSpec(memory_space=pltpu.VMEM)
SMEM = pl.BlockSpec(memory_space=pltpu.SMEM)


ANY = pl.BlockSpec(memory_space=pltpu.HBM)


def call(kernel, name, out, operands, scratch=(), vmem=24, scalars=False, where=0):
    return pl.pallas_call(
        kernel,
        out_shape=out,
        in_specs=[SMEM] * scalars + [ANY] * where + [VMEM] * (len(operands) - scalars - where),
        out_specs=jax.tree.map(lambda _: VMEM, out),
        scratch_shapes=list(scratch),
        compiler_params=pltpu.CompilerParams(vmem_limit_bytes=vmem << 20),
        name=name,
    )(*operands)


def local(tokens, in_weight, down_factors, up_factors, filters, task_ids, window_lengths, out_weight):
    f32, bf16 = jnp.float32, jnp.bfloat16
    segs, rows, depth = tokens.shape
    w_rows, _, channels = in_weight.shape
    ch = channels // 4
    windows = window_lengths.shape[1]
    ranks = segs * down_factors.shape[2]
    half = segs * rows
    count = segs * windows

    down, up = call(
        prepare_kernel,
        "adapters",
        (jax.ShapeDtypeStruct((ranks, depth), bf16), jax.ShapeDtypeStruct((ranks, 3 * ch), bf16)),
        (task_ids, down_factors.transpose(0, 2, 1), up_factors.transpose(0, 2, 1, 3)),
        [pltpu.SemaphoreType.DMA((8,))],
        scalars=True,
        where=2,
    )
    own = tokens.reshape(half, depth)
    other = x_pair_swap(own)
    spread = call(
        spread_kernel,
        "spread_weight",
        jax.ShapeDtypeStruct((8, w_rows, 3 * ch), bf16),
        (in_weight.transpose(1, 0, 2),),
    )
    spread, other = lax.optimization_barrier((spread, other))
    piece = call(
        join_kernel, "join_rows", jax.ShapeDtypeStruct((2 * half + ranks, depth), bf16), (own, other, down)
    )
    gathered = lax.all_gather(piece, ("zhi", "zlo"), axis=0, tiled=False)

    spread, piece = lax.optimization_barrier((spread, piece))
    met = lax.all_to_all(spread, ("xhi", "xlo", "zlo"), 0, 0, tiled=True)
    split = jax.ShapeDtypeStruct((4, w_rows, 3 * ch), bf16)
    kept, given = call(split_kernel, "split_rows", (split, split), (met,))
    weight = {0: jnp.stack([kept, core_swap(given)])}
    for step in range(1, NY // 2):
        weight[NY - step] = y_step(weight[(NY - step + 1) % NY], 1)
        weight[step] = y_step(weight[step - 1], -1)
    weight[NY // 2] = y_step(weight[NY // 2 + 1], 1)
    up_other = core_swap(up)

    cut = (4, half)
    features = w_rows * NY * 4
    early = [weight[d] for d in range(NY) if d != NY // 2]
    packed = call(
        pack_kernel,
        "pack_weights",
        jax.ShapeDtypeStruct((3, features, 2 * ch), bf16),
        tuple(early),
        [pltpu.VMEM((NY - 1, *weight[0].shape), bf16), pltpu.SemaphoreType.DMA((NY - 1,))],
        vmem=56,
        where=NY - 1,
    )
    low = call(low_kernel, "low_rank", jax.ShapeDtypeStruct((*cut, ranks), bf16), (gathered,))
    kv_own, kv_send, q_own, q_send = call(
        project_kernel,
        "project",
        (
            jax.ShapeDtypeStruct((*cut, 2 * ch), f32),
            jax.ShapeDtypeStruct((*cut, 2 * ch), bf16),
            jax.ShapeDtypeStruct((*cut, ch), f32),
            jax.ShapeDtypeStruct((*cut, ch), bf16),
        ),
        (gathered, packed, weight[NY // 2], low, up, up_other),
        [pltpu.VMEM(packed.shape, bf16)],
    )
    kv = call(
        combine_kernel,
        "combine_kv",
        jax.ShapeDtypeStruct((4, segs, rows, ch), bf16),
        (kv_own, core_swap(kv_send)),
    )
    wide, kv = lax.optimization_barrier((out_weight.T.astype(f32), kv))
    whole = lax.all_gather(wide, TENSOR, axis=0, tiled=True)
    prev = permute(kv, lambda x, y, z, c: (x, y + 1, z, c))
    wrap = permute(kv[3], lambda x, y, z, c: (x + 2, 0, z, c), lambda x, y, z, c: x < 2 and y == NY - 1)
    part = call(
        conv_own_kernel,
        "conv_own",
        jax.ShapeDtypeStruct((4, segs, rows, ch), f32),
        (kv, filters),
        [pltpu.VMEM((8 + rows, ch), f32), pltpu.VMEM((filters.shape[1], ch), f32)],
    )
    part, q_send = lax.optimization_barrier((part, q_send))
    q_met = core_swap(q_send)
    gate_scratch = [
        pltpu.VMEM((16 + rows, ch), f32),
        pltpu.VMEM((filters.shape[1], ch), f32),
        pltpu.VMEM((2, count, rows), jnp.int32),
    ]
    most = call(
        gate_most_kernel,
        "gate_most",
        jax.ShapeDtypeStruct((count, ch), f32),
        (window_lengths, part, q_own, q_met, prev, filters),
        gate_scratch,
        scalars=True,
    )
    total = call(
        gate_first_kernel,
        "gate_first",
        jax.ShapeDtypeStruct((NY, count, ch), bf16),
        (window_lengths, most, part, q_own, q_met, prev, wrap, filters),
        [*gate_scratch, pltpu.VMEM((count, ch), f32)],
        scalars=True,
    )

    met = lax.all_to_all(total, "y", 0, 0, tiled=True)
    total = call(sum_kernel, "sum_y", jax.ShapeDtypeStruct((8, 8, 8, ch), bf16), (met,))
    rest = TENSOR + ("xhi", "xlo", "zlo")
    met = lax.all_to_all(total.reshape(64, 8, ch), rest, 0, 0, tiled=True)
    met = met.reshape(8, 2, 4, 8, ch)
    out = call(
        embed_kernel,
        "embed",
        jax.ShapeDtypeStruct((8, out_weight.shape[1]), bf16),
        (window_lengths, met, whole),
        scalars=True,
    )
    return out.reshape(segs, windows // 8, out_weight.shape[1])


def solution(mesh):
    fine = Mesh(mesh.devices.reshape(SIZES), AXES)
    in_specs = (
        P(None, SEQ, TENSOR),
        P(SEQ, None, TENSOR),
        P(None, TENSOR, None),
        P(None, None, None, TENSOR),
        P(TENSOR, None),
        P(),
        P(),
        P(TENSOR, SEQ),
    )
    return jax.shard_map(local, mesh=fine, in_specs=in_specs, out_specs=P(None, TENSOR, SEQ), check_vma=False)
```

```python
import functools
import jax
import jax.numpy as jnp
from jax import lax
from jax.experimental import pallas as pl
from jax.experimental.pallas import tpu as pltpu
from jax.sharding import Mesh, PartitionSpec as P

AXES = ("xhi", "xlo", "zlo", "y", "zhi", "core")
SIZES = (2, 2, 2, 8, 4, 2)
SEQ = ("xhi", "xlo", "zlo", "y")
TENSOR = ("zhi", "core")
NZ, NY = 8, 8
adapter_scale = 0.5


def flat(x, y, z, c):
    return (((x % 4) * 2 + (z % NZ) % 2) * NY + y % NY) * 8 + ((z % NZ) // 2) * 2 + c


def permute(value, move, keep=lambda x, y, z, c: True):
    pairs = [
        (flat(x, y, z, c), flat(*move(x, y, z, c)))
        for x in range(4)
        for y in range(NY)
        for z in range(NZ)
        for c in range(2)
        if keep(x, y, z, c)
    ]
    return lax.ppermute(value, AXES, pairs)


def y_step(value, step):
    return permute(value, lambda x, y, z, c: (x, y + step, z, c))


def core_swap(value):
    return permute(value, lambda x, y, z, c: (x, y, z, 1 - c))


def x_pair_swap(value):
    return permute(value, lambda x, y, z, c: (x ^ 1, y, z, c))


def nt_dot(a, b):
    return lax.dot_general(a, b, (((1,), (1,)), ((), ())), preferred_element_type=jnp.float32)


def position():
    x_hi, x_lo, z_lo, y, z_hi, core = (lax.axis_index(name) for name in AXES)
    return x_hi, x_lo, z_lo, y, z_hi, core


def fetch(sources, targets, sems):
    copies = [pltpu.make_async_copy(a, b, sems.at[i]) for i, (a, b) in enumerate(zip(sources, targets))]
    for copy in copies:
        copy.start()
    for copy in copies:
        copy.wait()


def rows_of(tokens, quarter, half):
    x_lo, z_lo = quarter // 2, quarter % 2
    return jnp.concatenate([tokens[z, half * x_lo : half * (x_lo + 1), :] for z in range(z_lo, NZ, 2)], axis=1)


def place_rows(target, piece, y):
    _, blocks, w_rows, columns = piece.shape
    ch = columns // 3
    for block in range(blocks):
        at = pl.ds(pl.multiple_of((block * NY + y) * w_rows, w_rows), w_rows)
        for side in range(2):
            target[side, at, :] = piece[side, block, :, ch:]
            target[2, at, side * ch : (side + 1) * ch] = piece[side, block, :, :ch]


def pack_kernel(*refs):
    count = NY - 1
    out_ref, held, sems = refs[count:]
    copies = [pltpu.make_async_copy(refs[i], held.at[i], sems.at[i]) for i in range(count)]
    for copy in copies:
        copy.start()
    for i, dist in enumerate(d for d in range(NY) if d != NY // 2):
        copies[i].wait()
        place_rows(out_ref, held.at[i], lax.rem(position()[3] + dist, NY))


def low_kernel(tokens, packed, low_ref):
    _, half, ranks = low_ref.shape
    row = lax.broadcasted_iota(jnp.int32, (half, ranks), 0)
    column = lax.broadcasted_iota(jnp.int32, (half, ranks), 1)
    mine = (row >= half // 2) == (column >= ranks // 2)
    for quarter in range(4):
        down = jnp.concatenate([tokens[z, 2 * half :, :] for z in range(quarter % 2, NZ, 2)], axis=1)
        low = nt_dot(rows_of(tokens, quarter, half), down)
        low_ref[quarter] = jnp.where(mine, adapter_scale * low, 0.0).astype(low_ref.dtype)


def project_kernel(tokens, packed, last, low_ref, up, up_other, kv_own, kv_send, q_own, q_send, weight):
    weight[...] = packed[...]
    place_rows(weight, last, lax.rem(position()[3] + NY // 2, NY))
    half = kv_own.shape[1]
    ch = up.shape[1] // 3
    q_up = jnp.concatenate([up[:, :ch], up_other[:, :ch]], axis=1)
    for quarter in (0, 2, 1, 3):
        a = rows_of(tokens, quarter, half)
        low = low_ref[quarter]
        for side in range(2):
            part = jnp.dot(a, weight[side], preferred_element_type=jnp.float32)
            ups = (up if side == 0 else up_other)[:, ch:]
            part += jnp.dot(low, ups, preferred_element_type=jnp.float32)
            if side == 0:
                kv_own[quarter] = part
            else:
                kv_send[quarter] = part.astype(kv_send.dtype)
    for quarter in range(4):
        part = jnp.dot(rows_of(tokens, quarter, half), weight[2], preferred_element_type=jnp.float32)
        part += jnp.dot(low_ref[quarter], q_up, preferred_element_type=jnp.float32)
        q_own[quarter] = part[:, :ch]
        q_send[quarter] = part[:, ch:].astype(q_send.dtype)


def combine_kernel(own_ref, met_ref, kv_ref):
    rows, ch = kv_ref.shape[2], kv_ref.shape[3]
    for quarter in range(4):
        both = own_ref[quarter] + met_ref[quarter].astype(jnp.float32)
        kv = (both[:, :ch] * both[:, ch:]).astype(jnp.bfloat16)
        for seg in range(2):
            kv_ref[quarter, seg] = kv[rows * seg : rows * (seg + 1), :]


def prepare_kernel(tasks, down_ref, up_ref, down_out, up_out, sems):
    _, x_lo, z_lo, _, _, _ = position()
    ranks = down_ref.shape[1]
    ch = up_out.shape[1] // 3
    columns = pl.ds(pl.multiple_of((x_lo * 2 + z_lo) * ch, ch), ch)
    pairs = []
    for seg in range(2):
        at = pl.ds(seg * ranks, ranks)
        pairs.append((down_ref.at[tasks[seg]], down_out.at[at]))
        for stream in range(3):
            pairs.append((up_ref.at[tasks[seg], stream, :, columns], up_out.at[at, pl.ds(stream * ch, ch)]))
    fetch(*zip(*pairs), sems)


def join_kernel(own_ref, other_ref, down_ref, out_ref):
    x_lo = position()[1]
    half = own_ref.shape[0]
    out_ref[pl.ds(pl.multiple_of(x_lo * half, half), half), :] = own_ref[...]
    out_ref[pl.ds(pl.multiple_of((1 - x_lo) * half, half), half), :] = other_ref[...]
    out_ref[2 * half :, :] = down_ref[...]


def split_kernel(met_ref, kept_ref, given_ref):
    core = position()[5]
    for block in range(kept_ref.shape[0]):
        kept_ref[block] = met_ref[2 * block + core]
        given_ref[block] = met_ref[2 * block + 1 - core]


def spread_kernel(weight_ref, out_ref):
    ch = out_ref.shape[2] // 3
    for quarter in range(4):
        for stream in range(3):
            block = weight_ref[stream, :, quarter * ch : (quarter + 1) * ch]
            for copy in range(2):
                out_ref[copy * 4 + quarter, :, stream * ch : (stream + 1) * ch] = block


def spread_taps(taps_ref, tap, ch):
    return jnp.broadcast_to(taps_ref[tap : tap + 1, :], (8, ch))


def fill_taps(filters_ref, taps):
    _, x_lo, z_lo, _, _, _ = position()
    ch = taps.shape[1]
    mine = filters_ref[pl.ds(pl.multiple_of((x_lo * 2 + z_lo) * ch, ch), ch), :]
    taps[...] = mine.astype(jnp.float32).T


def conv_own_kernel(kv_ref, filters_ref, part_ref, ext, taps):
    rows, ch = kv_ref.shape[2], kv_ref.shape[3]
    groups = rows // 8
    fill_taps(filters_ref, taps)

    def block(n, carry):
        quarter, seg = n // 2, lax.rem(n, 2)
        ext[0:8, :] = jnp.zeros((8, ch), jnp.float32)
        ext[8:, :] = kv_ref[quarter, seg].astype(jnp.float32)
        total = [jnp.zeros((8, ch), jnp.float32) for _ in range(groups)]
        for r in range(8):
            shifted = [ext[8 * g + 8 - r : 8 * g + 16 - r, :] for g in range(groups)]
            for s in range(groups):
                tap = spread_taps(taps, 8 * s + r, ch)
                for g in range(s, groups):
                    total[g] = total[g] + tap * shifted[g - s]
        for g in range(groups):
            part_ref[quarter, seg, 8 * g : 8 * g + 8, :] = total[g]
        return carry

    lax.fori_loop(0, 8, block, 0)


def fill_edges(lengths, edges):
    each = lengths.shape[1] // 8
    for seg in range(2):
        start = jnp.int32(0)
        for window in range(lengths.shape[1]):
            at = (window // each) * 2 * each + seg * each + window % each
            end = start + lengths[seg, window]
            edges[0, at : at + 1, :] = jnp.full((1, edges.shape[2]), start, jnp.int32)
            edges[1, at : at + 1, :] = jnp.full((1, edges.shape[2]), end, jnp.int32)
            start = end


def gate_block(quarter, seg, before, part_ref, own_ref, met_ref, taps, edges, ext, sums):
    x_hi, _, _, y, _, _ = position()
    rows, ch = part_ref.shape[2], part_ref.shape[3]
    groups = rows // 8
    count = sums.shape[0]
    row = lax.broadcasted_iota(jnp.int32, (count, rows), 0)
    column = lax.broadcasted_iota(jnp.int32, (count, rows), 1)
    row_seg = lax.rem(row // 4, 2)
    ext[0:8, :] = jnp.zeros((8, ch), jnp.float32)
    ext[8 : 8 + rows, :] = before.astype(jnp.float32)
    ext[8 + rows :, :] = jnp.zeros((8, ch), jnp.float32)
    total = [part_ref[quarter, seg, 8 * g : 8 * g + 8, :] for g in range(groups)]
    for r in range(8):
        shifted = [ext[8 * g + 8 - r : 8 * g + 16 - r, :] for g in range(groups + (1 if r else 0))]
        for s in range(groups):
            tap = spread_taps(taps, 8 * s + r, ch)
            for g in range(groups):
                if groups + g - s < len(shifted):
                    total[g] = total[g] + tap * shifted[groups + g - s]
    at_rows = pl.ds(pl.multiple_of(seg * rows, rows), rows)
    q = own_ref[quarter, at_rows, :] + met_ref[quarter, at_rows, :].astype(jnp.float32)
    gated = (q * jnp.concatenate(total, axis=0)).astype(jnp.bfloat16)
    place = ((x_hi * 4 + quarter) * NY + y) * rows + column
    inside = (place >= edges[0]) & (place < edges[1]) & (row_seg == seg)
    member = inside.astype(jnp.float32).astype(jnp.bfloat16)
    sums[...] += jnp.dot(member, gated, preferred_element_type=jnp.float32)


def gate_most_kernel(lengths, part_ref, own_ref, met_ref, prev_ref, filters_ref, sums, ext, taps, edges):
    fill_taps(filters_ref, taps)
    fill_edges(lengths, edges)
    sums[...] = jnp.zeros(sums.shape, jnp.float32)
    y = position()[3]

    def block(n, carry):
        quarter, seg = n // 2, lax.rem(n, 2)
        before = prev_ref[jnp.where(y > 0, quarter, quarter - 1), seg]
        gate_block(quarter, seg, before, part_ref, own_ref, met_ref, taps, edges, ext, sums)
        return carry

    lax.fori_loop(2, 8, block, 0)


def gate_first_kernel(
    lengths, most_ref, part_ref, own_ref, met_ref, prev_ref, wrap_ref, filters_ref, out_ref, ext, taps, edges, sums
):
    fill_taps(filters_ref, taps)
    fill_edges(lengths, edges)
    sums[...] = most_ref[...]
    y = position()[3]

    def block(seg, carry):
        before = jnp.where(y > 0, prev_ref[0, seg].astype(jnp.float32), wrap_ref[seg].astype(jnp.float32))
        gate_block(0, seg, before, part_ref, own_ref, met_ref, taps, edges, ext, sums)
        return carry

    lax.fori_loop(0, 2, block, 0)
    for copy in range(out_ref.shape[0]):
        out_ref[copy] = sums[...].astype(out_ref.dtype)


def sum_kernel(met_ref, out_ref):
    total = met_ref[0].astype(jnp.float32)
    for i in range(1, met_ref.shape[0]):
        total = total + met_ref[i].astype(jnp.float32)
    rows = out_ref.shape[2]
    for place in range(out_ref.shape[0]):
        mine = total[place * rows : (place + 1) * rows, :].astype(out_ref.dtype)
        for copy in range(out_ref.shape[1]):
            out_ref[place, copy] = mine


def embed_kernel(lengths, met_ref, weight_ref, out_ref):
    _, _, _, _, z_hi, core = position()
    rows, ch = met_ref.shape[3], met_ref.shape[4]
    each = rows // 2
    row = lax.broadcasted_iota(jnp.int32, (rows, ch), 0)
    length = jnp.zeros((rows, ch), jnp.int32)
    for r in range(rows):
        length = jnp.where(row == r, lengths[r // each, (z_hi * 2 + core) * each + r % each], length)
    length = length.astype(jnp.float32)
    columns = weight_ref.shape[0] // met_ref.shape[0]
    total = jnp.zeros((rows, columns), jnp.float32)
    for t in range(met_ref.shape[0]):
        means = []
        for quarter in range(met_ref.shape[2]):
            both = met_ref[t, 0, quarter].astype(jnp.float32) + met_ref[t, 1, quarter].astype(jnp.float32)
            means.append((both / length).astype(jnp.bfloat16))
        weight = weight_ref[t * columns : (t + 1) * columns, :].astype(jnp.bfloat16)
        total += nt_dot(jnp.concatenate(means, axis=1), weight)
    out_ref[...] = total.astype(out_ref.dtype)


VMEM = pl.BlockSpec(memory_space=pltpu.VMEM)
SMEM = pl.BlockSpec(memory_space=pltpu.SMEM)


ANY = pl.BlockSpec(memory_space=pltpu.HBM)


def call(kernel, name, out, operands, scratch=(), vmem=24, scalars=False, where=0):
    return pl.pallas_call(
        kernel,
        out_shape=out,
        in_specs=[SMEM] * scalars + [ANY] * where + [VMEM] * (len(operands) - scalars - where),
        out_specs=jax.tree.map(lambda _: VMEM, out),
        scratch_shapes=list(scratch),
        compiler_params=pltpu.CompilerParams(vmem_limit_bytes=vmem << 20),
        name=name,
    )(*operands)


def local(tokens, in_weight, down_factors, up_factors, filters, task_ids, window_lengths, out_weight):
    f32, bf16 = jnp.float32, jnp.bfloat16
    segs, rows, depth = tokens.shape
    w_rows, _, channels = in_weight.shape
    ch = channels // 4
    windows = window_lengths.shape[1]
    ranks = segs * down_factors.shape[2]
    half = segs * rows
    count = segs * windows

    down, up = call(
        prepare_kernel,
        "adapters",
        (jax.ShapeDtypeStruct((ranks, depth), bf16), jax.ShapeDtypeStruct((ranks, 3 * ch), bf16)),
        (task_ids, down_factors.transpose(0, 2, 1), up_factors.transpose(0, 2, 1, 3)),
        [pltpu.SemaphoreType.DMA((8,))],
        scalars=True,
        where=2,
    )
    own = tokens.reshape(half, depth)
    other = x_pair_swap(own)
    spread = call(
        spread_kernel,
        "spread_weight",
        jax.ShapeDtypeStruct((8, w_rows, 3 * ch), bf16),
        (in_weight.transpose(1, 0, 2),),
    )
    spread, other = lax.optimization_barrier((spread, other))
    piece = call(
        join_kernel, "join_rows", jax.ShapeDtypeStruct((2 * half + ranks, depth), bf16), (own, other, down)
    )
    gathered = lax.all_gather(piece, ("zhi", "zlo"), axis=0, tiled=False)

    spread, piece = lax.optimization_barrier((spread, piece))
    met = lax.all_to_all(spread, ("xhi", "xlo", "zlo"), 0, 0, tiled=True)
    split = jax.ShapeDtypeStruct((4, w_rows, 3 * ch), bf16)
    kept, given = call(split_kernel, "split_rows", (split, split), (met,))
    weight = {0: jnp.stack([kept, core_swap(given)])}
    for step in range(1, NY // 2):
        weight[NY - step] = y_step(weight[(NY - step + 1) % NY], 1)
        weight[step] = y_step(weight[step - 1], -1)
    weight[NY // 2] = y_step(weight[NY // 2 + 1], 1)
    up_other = core_swap(up)

    cut = (4, half)
    features = w_rows * NY * 4
    early = [weight[d] for d in range(NY) if d != NY // 2]
    packed = call(
        pack_kernel,
        "pack_weights",
        jax.ShapeDtypeStruct((3, features, 2 * ch), bf16),
        tuple(early),
        [pltpu.VMEM((NY - 1, *weight[0].shape), bf16), pltpu.SemaphoreType.DMA((NY - 1,))],
        vmem=56,
        where=NY - 1,
    )
    low = call(low_kernel, "low_rank", jax.ShapeDtypeStruct((*cut, ranks), bf16), (gathered, packed))
    kv_own, kv_send, q_own, q_send = call(
        project_kernel,
        "project",
        (
            jax.ShapeDtypeStruct((*cut, 2 * ch), f32),
            jax.ShapeDtypeStruct((*cut, 2 * ch), bf16),
            jax.ShapeDtypeStruct((*cut, ch), f32),
            jax.ShapeDtypeStruct((*cut, ch), bf16),
        ),
        (gathered, packed, weight[NY // 2], low, up, up_other),
        [pltpu.VMEM(packed.shape, bf16)],
    )
    kv = call(
        combine_kernel,
        "combine_kv",
        jax.ShapeDtypeStruct((4, segs, rows, ch), bf16),
        (kv_own, core_swap(kv_send)),
    )
    wide, kv = lax.optimization_barrier((out_weight.T.astype(f32), kv))
    whole = lax.all_gather(wide, TENSOR, axis=0, tiled=True)
    prev = permute(kv, lambda x, y, z, c: (x, y + 1, z, c))
    wrap = permute(kv[3], lambda x, y, z, c: (x + 2, 0, z, c), lambda x, y, z, c: x < 2 and y == NY - 1)
    part = call(
        conv_own_kernel,
        "conv_own",
        jax.ShapeDtypeStruct((4, segs, rows, ch), f32),
        (kv, filters),
        [pltpu.VMEM((8 + rows, ch), f32), pltpu.VMEM((filters.shape[1], ch), f32)],
    )
    part, q_send = lax.optimization_barrier((part, q_send))
    q_met = core_swap(q_send)
    gate_scratch = [
        pltpu.VMEM((16 + rows, ch), f32),
        pltpu.VMEM((filters.shape[1], ch), f32),
        pltpu.VMEM((2, count, rows), jnp.int32),
    ]
    most = call(
        gate_most_kernel,
        "gate_most",
        jax.ShapeDtypeStruct((count, ch), f32),
        (window_lengths, part, q_own, q_met, prev, filters),
        gate_scratch,
        scalars=True,
    )
    total = call(
        gate_first_kernel,
        "gate_first",
        jax.ShapeDtypeStruct((NY, count, ch), bf16),
        (window_lengths, most, part, q_own, q_met, prev, wrap, filters),
        [*gate_scratch, pltpu.VMEM((count, ch), f32)],
        scalars=True,
    )

    met = lax.all_to_all(total, "y", 0, 0, tiled=True)
    total = call(sum_kernel, "sum_y", jax.ShapeDtypeStruct((8, 8, 8, ch), bf16), (met,))
    rest = TENSOR + ("xhi", "xlo", "zlo")
    met = lax.all_to_all(total.reshape(64, 8, ch), rest, 0, 0, tiled=True)
    met = met.reshape(8, 2, 4, 8, ch)
    out = call(
        embed_kernel,
        "embed",
        jax.ShapeDtypeStruct((8, out_weight.shape[1]), bf16),
        (window_lengths, met, whole),
        scalars=True,
    )
    return out.reshape(segs, windows // 8, out_weight.shape[1])


def solution(mesh):
    fine = Mesh(mesh.devices.reshape(SIZES), AXES)
    in_specs = (
        P(None, SEQ, TENSOR),
        P(SEQ, None, TENSOR),
        P(None, TENSOR, None),
        P(None, None, None, TENSOR),
        P(TENSOR, None),
        P(),
        P(),
        P(TENSOR, SEQ),
    )
    return jax.shard_map(local, mesh=fine, in_specs=in_specs, out_specs=P(None, TENSOR, SEQ), check_vma=False)
```

```python
import functools
import jax
import jax.numpy as jnp
from jax import lax
from jax.experimental import pallas as pl
from jax.experimental.pallas import tpu as pltpu
from jax.sharding import Mesh, PartitionSpec as P

AXES = ("xhi", "xlo", "zlo", "y", "zhi", "core")
SIZES = (2, 2, 2, 8, 4, 2)
SEQ = ("xhi", "xlo", "zlo", "y")
TENSOR = ("zhi", "core")
NZ, NY = 8, 8
adapter_scale = 0.5


def flat(x, y, z, c):
    return (((x % 4) * 2 + (z % NZ) % 2) * NY + y % NY) * 8 + ((z % NZ) // 2) * 2 + c


def permute(value, move, keep=lambda x, y, z, c: True):
    pairs = [
        (flat(x, y, z, c), flat(*move(x, y, z, c)))
        for x in range(4)
        for y in range(NY)
        for z in range(NZ)
        for c in range(2)
        if keep(x, y, z, c)
    ]
    return lax.ppermute(value, AXES, pairs)


def y_step(value, step):
    return permute(value, lambda x, y, z, c: (x, y + step, z, c))


def core_swap(value):
    return permute(value, lambda x, y, z, c: (x, y, z, 1 - c))


def x_pair_swap(value):
    return permute(value, lambda x, y, z, c: (x ^ 1, y, z, c))


def nt_dot(a, b):
    return lax.dot_general(a, b, (((1,), (1,)), ((), ())), preferred_element_type=jnp.float32)


def position():
    x_hi, x_lo, z_lo, y, z_hi, core = (lax.axis_index(name) for name in AXES)
    return x_hi, x_lo, z_lo, y, z_hi, core


def fetch(sources, targets, sems):
    copies = [pltpu.make_async_copy(a, b, sems.at[i]) for i, (a, b) in enumerate(zip(sources, targets))]
    for copy in copies:
        copy.start()
    for copy in copies:
        copy.wait()


def rows_of(tokens, quarter, half):
    x_lo, z_lo = quarter // 2, quarter % 2
    return jnp.concatenate([tokens[z, half * x_lo : half * (x_lo + 1), :] for z in range(z_lo, NZ, 2)], axis=1)


def place_rows(target, piece, y):
    _, blocks, w_rows, columns = piece.shape
    ch = columns // 3
    for block in range(blocks):
        at = pl.ds(pl.multiple_of((block * NY + y) * w_rows, w_rows), w_rows)
        for side in range(2):
            target[side, at, :] = piece[side, block, :, ch:]
            target[2, at, side * ch : (side + 1) * ch] = piece[side, block, :, :ch]


def pack_kernel(*refs):
    count = NY - 1
    out_ref, held, sems = refs[count:]
    copies = [pltpu.make_async_copy(refs[i], held.at[i], sems.at[i]) for i in range(count)]
    for copy in copies:
        copy.start()
    for i, dist in enumerate(d for d in range(NY) if d != NY // 2):
        copies[i].wait()
        place_rows(out_ref, held.at[i], lax.rem(position()[3] + dist, NY))


def low_kernel(tokens, low_ref):
    _, half, ranks = low_ref.shape
    row = lax.broadcasted_iota(jnp.int32, (half, ranks), 0)
    column = lax.broadcasted_iota(jnp.int32, (half, ranks), 1)
    mine = (row >= half // 2) == (column >= ranks // 2)
    for quarter in range(4):
        down = jnp.concatenate([tokens[z, 2 * half :, :] for z in range(quarter % 2, NZ, 2)], axis=1)
        low = nt_dot(rows_of(tokens, quarter, half), down)
        low_ref[quarter] = jnp.where(mine, adapter_scale * low, 0.0).astype(low_ref.dtype)


def project_kernel(tokens, packed, last, low_ref, up, up_other, kv_own, kv_send, q_own, q_send, weight):
    weight[...] = packed[...]
    place_rows(weight, last, lax.rem(position()[3] + NY // 2, NY))
    half = kv_own.shape[1]
    ch = up.shape[1] // 3
    q_up = jnp.concatenate([up[:, :ch], up_other[:, :ch]], axis=1)
    for quarter in (0, 2, 1, 3):
        a = rows_of(tokens, quarter, half)
        low = low_ref[quarter]
        for side in range(2):
            part = jnp.dot(a, weight[side], preferred_element_type=jnp.float32)
            ups = (up if side == 0 else up_other)[:, ch:]
            part += jnp.dot(low, ups, preferred_element_type=jnp.float32)
            if side == 0:
                kv_own[quarter] = part
            else:
                kv_send[quarter] = part.astype(kv_send.dtype)
    for quarter in range(4):
        part = jnp.dot(rows_of(tokens, quarter, half), weight[2], preferred_element_type=jnp.float32)
        part += jnp.dot(low_ref[quarter], q_up, preferred_element_type=jnp.float32)
        q_own[quarter] = part[:, :ch]
        q_send[quarter] = part[:, ch:].astype(q_send.dtype)


def combine_kernel(own_ref, met_ref, kv_ref):
    rows, ch = kv_ref.shape[2], kv_ref.shape[3]
    for quarter in range(4):
        both = own_ref[quarter] + met_ref[quarter].astype(jnp.float32)
        kv = (both[:, :ch] * both[:, ch:]).astype(jnp.bfloat16)
        for seg in range(2):
            kv_ref[quarter, seg] = kv[rows * seg : rows * (seg + 1), :]


def prepare_kernel(tasks, down_ref, up_ref, down_out, up_out, sems):
    _, x_lo, z_lo, _, _, _ = position()
    ranks = down_ref.shape[1]
    ch = up_out.shape[1] // 3
    columns = pl.ds(pl.multiple_of((x_lo * 2 + z_lo) * ch, ch), ch)
    pairs = []
    for seg in range(2):
        at = pl.ds(seg * ranks, ranks)
        pairs.append((down_ref.at[tasks[seg]], down_out.at[at]))
        for stream in range(3):
            pairs.append((up_ref.at[tasks[seg], stream, :, columns], up_out.at[at, pl.ds(stream * ch, ch)]))
    fetch(*zip(*pairs), sems)


def join_kernel(own_ref, other_ref, down_ref, out_ref):
    x_lo = position()[1]
    half = own_ref.shape[0]
    out_ref[pl.ds(pl.multiple_of(x_lo * half, half), half), :] = own_ref[...]
    out_ref[pl.ds(pl.multiple_of((1 - x_lo) * half, half), half), :] = other_ref[...]
    out_ref[2 * half :, :] = down_ref[...]


def split_kernel(met_ref, kept_ref, given_ref):
    core = position()[5]
    for block in range(kept_ref.shape[0]):
        kept_ref[block] = met_ref[2 * block + core]
        given_ref[block] = met_ref[2 * block + 1 - core]


def spread_kernel(weight_ref, own_ref, out_ref, rows_ref):
    rows_ref[...] = own_ref[...]
    ch = out_ref.shape[2] // 3
    for quarter in range(4):
        for stream in range(3):
            block = weight_ref[stream, :, quarter * ch : (quarter + 1) * ch]
            for copy in range(2):
                out_ref[copy * 4 + quarter, :, stream * ch : (stream + 1) * ch] = block


def spread_taps(taps_ref, tap, ch):
    return jnp.broadcast_to(taps_ref[tap : tap + 1, :], (8, ch))


def fill_taps(filters_ref, taps):
    _, x_lo, z_lo, _, _, _ = position()
    ch = taps.shape[1]
    mine = filters_ref[pl.ds(pl.multiple_of((x_lo * 2 + z_lo) * ch, ch), ch), :]
    taps[...] = mine.astype(jnp.float32).T


def conv_own_kernel(kv_ref, filters_ref, part_ref, ext, taps):
    rows, ch = kv_ref.shape[2], kv_ref.shape[3]
    groups = rows // 8
    fill_taps(filters_ref, taps)

    def block(n, carry):
        quarter, seg = n // 2, lax.rem(n, 2)
        ext[0:8, :] = jnp.zeros((8, ch), jnp.float32)
        ext[8:, :] = kv_ref[quarter, seg].astype(jnp.float32)
        total = [jnp.zeros((8, ch), jnp.float32) for _ in range(groups)]
        for r in range(8):
            shifted = [ext[8 * g + 8 - r : 8 * g + 16 - r, :] for g in range(groups)]
            for s in range(groups):
                tap = spread_taps(taps, 8 * s + r, ch)
                for g in range(s, groups):
                    total[g] = total[g] + tap * shifted[g - s]
        for g in range(groups):
            part_ref[quarter, seg, 8 * g : 8 * g + 8, :] = total[g]
        return carry

    lax.fori_loop(0, 8, block, 0)


def fill_edges(lengths, edges):
    each = lengths.shape[1] // 8
    for seg in range(2):
        start = jnp.int32(0)
        for window in range(lengths.shape[1]):
            at = (window // each) * 2 * each + seg * each + window % each
            end = start + lengths[seg, window]
            edges[0, at : at + 1, :] = jnp.full((1, edges.shape[2]), start, jnp.int32)
            edges[1, at : at + 1, :] = jnp.full((1, edges.shape[2]), end, jnp.int32)
            start = end


def gate_block(quarter, seg, before, part_ref, own_ref, met_ref, taps, edges, ext, sums):
    x_hi, _, _, y, _, _ = position()
    rows, ch = part_ref.shape[2], part_ref.shape[3]
    groups = rows // 8
    count = sums.shape[0]
    row = lax.broadcasted_iota(jnp.int32, (count, rows), 0)
    column = lax.broadcasted_iota(jnp.int32, (count, rows), 1)
    row_seg = lax.rem(row // 4, 2)
    ext[0:8, :] = jnp.zeros((8, ch), jnp.float32)
    ext[8 : 8 + rows, :] = before.astype(jnp.float32)
    ext[8 + rows :, :] = jnp.zeros((8, ch), jnp.float32)
    total = [part_ref[quarter, seg, 8 * g : 8 * g + 8, :] for g in range(groups)]
    for r in range(8):
        shifted = [ext[8 * g + 8 - r : 8 * g + 16 - r, :] for g in range(groups + (1 if r else 0))]
        for s in range(groups):
            tap = spread_taps(taps, 8 * s + r, ch)
            for g in range(groups):
                if groups + g - s < len(shifted):
                    total[g] = total[g] + tap * shifted[groups + g - s]
    at_rows = pl.ds(pl.multiple_of(seg * rows, rows), rows)
    q = own_ref[quarter, at_rows, :] + met_ref[quarter, at_rows, :].astype(jnp.float32)
    gated = (q * jnp.concatenate(total, axis=0)).astype(jnp.bfloat16)
    place = ((x_hi * 4 + quarter) * NY + y) * rows + column
    inside = (place >= edges[0]) & (place < edges[1]) & (row_seg == seg)
    member = inside.astype(jnp.float32).astype(jnp.bfloat16)
    sums[...] += jnp.dot(member, gated, preferred_element_type=jnp.float32)


def gate_most_kernel(lengths, part_ref, own_ref, met_ref, prev_ref, filters_ref, sums, ext, taps, edges):
    fill_taps(filters_ref, taps)
    fill_edges(lengths, edges)
    sums[...] = jnp.zeros(sums.shape, jnp.float32)
    y = position()[3]

    def block(n, carry):
        quarter, seg = n // 2, lax.rem(n, 2)
        before = prev_ref[jnp.where(y > 0, quarter, quarter - 1), seg]
        gate_block(quarter, seg, before, part_ref, own_ref, met_ref, taps, edges, ext, sums)
        return carry

    lax.fori_loop(2, 8, block, 0)


def gate_first_kernel(
    lengths, most_ref, part_ref, own_ref, met_ref, prev_ref, wrap_ref, filters_ref, out_ref, ext, taps, edges, sums
):
    fill_taps(filters_ref, taps)
    fill_edges(lengths, edges)
    sums[...] = most_ref[...]
    y = position()[3]

    def block(seg, carry):
        before = jnp.where(y > 0, prev_ref[0, seg].astype(jnp.float32), wrap_ref[seg].astype(jnp.float32))
        gate_block(0, seg, before, part_ref, own_ref, met_ref, taps, edges, ext, sums)
        return carry

    lax.fori_loop(0, 2, block, 0)
    for copy in range(out_ref.shape[0]):
        out_ref[copy] = sums[...].astype(out_ref.dtype)


def sum_kernel(met_ref, out_ref):
    total = met_ref[0].astype(jnp.float32)
    for i in range(1, met_ref.shape[0]):
        total = total + met_ref[i].astype(jnp.float32)
    rows = out_ref.shape[2]
    for place in range(out_ref.shape[0]):
        mine = total[place * rows : (place + 1) * rows, :].astype(out_ref.dtype)
        for copy in range(out_ref.shape[1]):
            out_ref[place, copy] = mine


def embed_kernel(lengths, met_ref, weight_ref, out_ref):
    _, _, _, _, z_hi, core = position()
    rows, ch = met_ref.shape[3], met_ref.shape[4]
    each = rows // 2
    row = lax.broadcasted_iota(jnp.int32, (rows, ch), 0)
    length = jnp.zeros((rows, ch), jnp.int32)
    for r in range(rows):
        length = jnp.where(row == r, lengths[r // each, (z_hi * 2 + core) * each + r % each], length)
    length = length.astype(jnp.float32)
    columns = weight_ref.shape[0] // met_ref.shape[0]
    total = jnp.zeros((rows, columns), jnp.float32)
    for t in range(met_ref.shape[0]):
        means = []
        for quarter in range(met_ref.shape[2]):
            both = met_ref[t, 0, quarter].astype(jnp.float32) + met_ref[t, 1, quarter].astype(jnp.float32)
            means.append((both / length).astype(jnp.bfloat16))
        weight = weight_ref[t * columns : (t + 1) * columns, :].astype(jnp.bfloat16)
        total += nt_dot(jnp.concatenate(means, axis=1), weight)
    out_ref[...] = total.astype(out_ref.dtype)


VMEM = pl.BlockSpec(memory_space=pltpu.VMEM)
SMEM = pl.BlockSpec(memory_space=pltpu.SMEM)


ANY = pl.BlockSpec(memory_space=pltpu.HBM)


def call(kernel, name, out, operands, scratch=(), vmem=24, scalars=False, where=0):
    return pl.pallas_call(
        kernel,
        out_shape=out,
        in_specs=[SMEM] * scalars + [ANY] * where + [VMEM] * (len(operands) - scalars - where),
        out_specs=jax.tree.map(lambda _: VMEM, out),
        scratch_shapes=list(scratch),
        compiler_params=pltpu.CompilerParams(vmem_limit_bytes=vmem << 20),
        name=name,
    )(*operands)


def local(tokens, in_weight, down_factors, up_factors, filters, task_ids, window_lengths, out_weight):
    f32, bf16 = jnp.float32, jnp.bfloat16
    segs, rows, depth = tokens.shape
    w_rows, _, channels = in_weight.shape
    ch = channels // 4
    windows = window_lengths.shape[1]
    ranks = segs * down_factors.shape[2]
    half = segs * rows
    count = segs * windows

    down, up = call(
        prepare_kernel,
        "adapters",
        (jax.ShapeDtypeStruct((ranks, depth), bf16), jax.ShapeDtypeStruct((ranks, 3 * ch), bf16)),
        (task_ids, down_factors.transpose(0, 2, 1), up_factors.transpose(0, 2, 1, 3)),
        [pltpu.SemaphoreType.DMA((8,))],
        scalars=True,
        where=2,
    )
    own = tokens.reshape(half, depth)
    other = x_pair_swap(own)
    spread, own_rows = call(
        spread_kernel,
        "spread_weight",
        (jax.ShapeDtypeStruct((8, w_rows, 3 * ch), bf16), jax.ShapeDtypeStruct(own.shape, bf16)),
        (in_weight.transpose(1, 0, 2), own),
    )
    spread, own_rows, other = lax.optimization_barrier((spread, own_rows, other))
    piece = call(
        join_kernel, "join_rows", jax.ShapeDtypeStruct((2 * half + ranks, depth), bf16), (own_rows, other, down)
    )
    gathered = lax.all_gather(piece, ("zhi", "zlo"), axis=0, tiled=False)

    spread, piece = lax.optimization_barrier((spread, piece))
    met = lax.all_to_all(spread, ("xhi", "xlo", "zlo"), 0, 0, tiled=True)
    split = jax.ShapeDtypeStruct((4, w_rows, 3 * ch), bf16)
    kept, given = call(split_kernel, "split_rows", (split, split), (met,))
    weight = {0: jnp.stack([kept, core_swap(given)])}
    for step in range(1, NY // 2):
        weight[NY - step] = y_step(weight[(NY - step + 1) % NY], 1)
        weight[step] = y_step(weight[step - 1], -1)
    weight[NY // 2] = y_step(weight[NY // 2 + 1], 1)
    up_other = core_swap(up)

    cut = (4, half)
    features = w_rows * NY * 4
    early = [weight[d] for d in range(NY) if d != NY // 2]
    packed = call(
        pack_kernel,
        "pack_weights",
        jax.ShapeDtypeStruct((3, features, 2 * ch), bf16),
        tuple(early),
        [pltpu.VMEM((NY - 1, *weight[0].shape), bf16), pltpu.SemaphoreType.DMA((NY - 1,))],
        vmem=56,
        where=NY - 1,
    )
    low = call(low_kernel, "low_rank", jax.ShapeDtypeStruct((*cut, ranks), bf16), (gathered,))
    kv_own, kv_send, q_own, q_send = call(
        project_kernel,
        "project",
        (
            jax.ShapeDtypeStruct((*cut, 2 * ch), f32),
            jax.ShapeDtypeStruct((*cut, 2 * ch), bf16),
            jax.ShapeDtypeStruct((*cut, ch), f32),
            jax.ShapeDtypeStruct((*cut, ch), bf16),
        ),
        (gathered, packed, weight[NY // 2], low, up, up_other),
        [pltpu.VMEM(packed.shape, bf16)],
    )
    kv = call(
        combine_kernel,
        "combine_kv",
        jax.ShapeDtypeStruct((4, segs, rows, ch), bf16),
        (kv_own, core_swap(kv_send)),
    )
    wide, kv = lax.optimization_barrier((out_weight.T.astype(f32), kv))
    whole = lax.all_gather(wide, TENSOR, axis=0, tiled=True)
    prev = permute(kv, lambda x, y, z, c: (x, y + 1, z, c))
    wrap = permute(kv[3], lambda x, y, z, c: (x + 2, 0, z, c), lambda x, y, z, c: x < 2 and y == NY - 1)
    part = call(
        conv_own_kernel,
        "conv_own",
        jax.ShapeDtypeStruct((4, segs, rows, ch), f32),
        (kv, filters),
        [pltpu.VMEM((8 + rows, ch), f32), pltpu.VMEM((filters.shape[1], ch), f32)],
    )
    part, q_send = lax.optimization_barrier((part, q_send))
    q_met = core_swap(q_send)
    gate_scratch = [
        pltpu.VMEM((16 + rows, ch), f32),
        pltpu.VMEM((filters.shape[1], ch), f32),
        pltpu.VMEM((2, count, rows), jnp.int32),
    ]
    most = call(
        gate_most_kernel,
        "gate_most",
        jax.ShapeDtypeStruct((count, ch), f32),
        (window_lengths, part, q_own, q_met, prev, filters),
        gate_scratch,
        scalars=True,
    )
    total = call(
        gate_first_kernel,
        "gate_first",
        jax.ShapeDtypeStruct((NY, count, ch), bf16),
        (window_lengths, most, part, q_own, q_met, prev, wrap, filters),
        [*gate_scratch, pltpu.VMEM((count, ch), f32)],
        scalars=True,
    )

    met = lax.all_to_all(total, "y", 0, 0, tiled=True)
    total = call(sum_kernel, "sum_y", jax.ShapeDtypeStruct((8, 8, 8, ch), bf16), (met,))
    rest = TENSOR + ("xhi", "xlo", "zlo")
    met = lax.all_to_all(total.reshape(64, 8, ch), rest, 0, 0, tiled=True)
    met = met.reshape(8, 2, 4, 8, ch)
    out = call(
        embed_kernel,
        "embed",
        jax.ShapeDtypeStruct((8, out_weight.shape[1]), bf16),
        (window_lengths, met, whole),
        scalars=True,
    )
    return out.reshape(segs, windows // 8, out_weight.shape[1])


def solution(mesh):
    fine = Mesh(mesh.devices.reshape(SIZES), AXES)
    in_specs = (
        P(None, SEQ, TENSOR),
        P(SEQ, None, TENSOR),
        P(None, TENSOR, None),
        P(None, None, None, TENSOR),
        P(TENSOR, None),
        P(),
        P(),
        P(TENSOR, SEQ),
    )
    return jax.shard_map(local, mesh=fine, in_specs=in_specs, out_specs=P(None, TENSOR, SEQ), check_vma=False)
```
